256 devices in a mesh: sec: 2 (over z_hi), rcv: 128 (over y, z_lo, x, core).
Axes of the slice: x: 4, y: 4, z: 8 (z_hi: 2, z_lo: 4; z = z_hi * 4 + z_lo), core: 2. Of those that a mesh axis runs over, the one named last changes fastest.
Arguments:
- strain: float32 [16384, 8192], P('rcv', 'sec'), may hold values from -6 to 6
- offset: int32 [16384], P('rcv'), may hold values from 0 to 3
- fir_taps: float32 [64], replicated, may hold values from -0.75 to 0.75
- source_channel: int32 [256], P('rcv'), may hold values from 0 to 127
Outputs:
- correlations: bfloat16 [2, 128, 16384, 128], P('sec', None, 'rcv')
The draws below stay inside these ranges and needn't reach their ends.
All inputs are finite; a program needn't handle non-finite values.
Results may differ from the reference program's by a relative error of at most 0.0068.
Values may be sent and summed in bfloat16 or wider, within the bound.
No kernel may reach another device: no remote copies, remote signals or barrier semaphores. Data moves between devices by JAX's collectives and lax.ppermute only.
A program may use at most 128 MiB of HBM per device.

```python
import math
import jax
import jax.numpy as jnp
from jax import lax

CH_DEV = 128
SRC_DEV = 2
TD = 2048
STRIDE = 4
TAPS = 64
BAND = 64
LAGS = 128
CH = 16384
NBLK = 128
NV = 256
TR = 8192
FREQ = 1024


def touch_ends(entries, rng, smallest, largest):
    longest = entries.shape.index(max(entries.shape))
    spots = []
    for shift in (0, 1):
        where = [jax.random.randint(jax.random.fold_in(rng, axis), (), 0, length) for axis, length in enumerate(entries.shape)]
        where[longest] = (where[longest] + shift) % entries.shape[longest]
        spots.append(tuple(where))
    return entries.at[spots[0]].set(smallest).at[spots[1]].set(largest)


def steps_of(key, dims, split, smallest, high):
    factor_of = 1.0
    for position, blocks in split:
        steps = jax.random.uniform(jax.random.fold_in(jax.random.fold_in(key, 6), position), (blocks,), jnp.float32, smallest / len(split), high / len(split))
        factor_of = factor_of * jnp.repeat(jnp.exp(steps), dims[position] // blocks).reshape((-1,) + (1,) * (len(dims) - 1 - position))
    return factor_of


def scatter_about(own_key, extent, deviation, bound, pieces=(), kind=jnp.bfloat16):
    factor_of = steps_of(own_key, extent, pieces, -0.22, 0.18) if pieces else 1.0
    values = jax.random.normal(own_key, extent, jnp.float32) * deviation * factor_of
    return jnp.minimum(jnp.maximum(values, -bound), bound).astype(kind)


def setup_inputs(seed: int = 0) -> dict:
    arg_keys = jax.random.split(jax.random.key(seed), 5)
    return {
        "strain": scatter_about(arg_keys[0], (CH, TR), 1.0, 6.0, ((0, 128), (1, 2)), jnp.float32),
        "offset": touch_ends(jax.random.randint(arg_keys[1], (CH,), 0, STRIDE), jax.random.fold_in(arg_keys[1], 1), 0, STRIDE - 1).astype(jnp.int32),
        "fir_taps": scatter_about(arg_keys[2], (TAPS,), TAPS ** -0.5, 0.75, (), jnp.float32),
        "source_channel": touch_ends(jax.random.randint(arg_keys[3], (NV,), 0, CH_DEV), jax.random.fold_in(arg_keys[3], 1), 0, CH_DEV - 1).astype(jnp.int32),
    }


def fir_weights(fir_taps, offset):
    shift_count = TAPS // STRIDE + 1
    phases = jnp.arange(STRIDE, dtype=jnp.int32)
    shifts = jnp.arange(shift_count, dtype=jnp.int32)
    tap_index = TAPS + phases[:, None, None] - STRIDE * shifts[None, :, None] - phases[None, None, :]
    matches = (tap_index[..., None] == jnp.arange(TAPS, dtype=jnp.int32)).astype(jnp.float32)
    per_phase = lax.optimization_barrier(jnp.sum(matches * fir_taps, axis=-1))
    selector = (offset[:, None] == phases[None, :]).astype(jnp.float32)
    return jnp.einsum('co,oms->cms', selector, per_phase, precision=lax.Precision.HIGHEST)

def decimate(extended, weights, samples):
    channels = extended.shape[0]
    frames = extended.reshape(channels, -1, STRIDE).transpose(0, 2, 1)
    filtered = jnp.zeros((channels, samples), jnp.float32)
    for shift_pos in range(weights.shape[1]):
        for phase in range(STRIDE):
            filtered = filtered + weights[:, shift_pos, phase, None] * frames[:, phase, shift_pos:shift_pos + samples]
    return filtered

def row_parts(row_ids, first_half):
    half_bins = FREQ // 2
    half_id = first_half + row_ids // FREQ
    component = row_ids % FREQ // half_bins
    freq_id = half_id * half_bins + row_ids % half_bins
    return (component, freq_id)

def spectrum_block(row_ids, time_ids, traces):
    component, freq_id = row_parts(row_ids, 0)
    phase_ids = freq_id[:, None] * time_ids[None, :] % TD
    angles = 2.0 * math.pi / TD * phase_ids.astype(jnp.float32)
    dft_table = jnp.where(component[:, None] == 0, jnp.cos(angles), -jnp.sin(angles))
    return lax.dot_general(dft_table, traces, (((1,), (1,)), ((), ())), precision=lax.Precision.HIGHEST, preferred_element_type=jnp.float32)

def whiten(spectra):
    halves = spectra.shape[0] // FREQ
    channels = spectra.shape[1]
    shaped = spectra.reshape(halves, 2, FREQ // 2 // BAND, BAND, channels)
    band_power = lax.optimization_barrier(jnp.mean(shaped * shaped, axis=(1, 3), keepdims=True))
    return (shaped / jnp.sqrt(band_power + 1e-06)).reshape(spectra.shape).astype(jnp.bfloat16)

def lag_table(row_ids, first_half):
    component, freq_id = row_parts(row_ids, first_half)
    lag_ids = jnp.arange(LAGS, dtype=jnp.int32) - LAGS // 2
    phase_ids = freq_id[:, None] * lag_ids[None, :] % TD
    angles = 2.0 * math.pi / TD * phase_ids.astype(jnp.float32)
    return jnp.where(component[:, None] == 0, jnp.cos(angles), -jnp.sin(angles)).astype(jnp.bfloat16)

def cross_block(sources, receivers):
    block_size, row_count = sources.shape
    channels = receivers.shape[1]
    halves = row_count // FREQ
    half_bins = FREQ // 2
    source = sources.reshape(block_size, halves, 2, half_bins).astype(jnp.float32)
    receiver = receivers.reshape(halves, 2, half_bins, channels).astype(jnp.float32)
    cross_re = source[:, :, 0, :, None] * receiver[None, :, 0] + source[:, :, 1, :, None] * receiver[None, :, 1]
    cross_im = source[:, :, 0, :, None] * receiver[None, :, 1] - source[:, :, 1, :, None] * receiver[None, :, 0]
    return jnp.stack([cross_re, cross_im], axis=2).reshape(block_size, row_count, channels).astype(jnp.bfloat16)

def reference(strain, offset, fir_taps, source_channel):
    channels = strain.shape[0]
    extended = jnp.concatenate([jnp.zeros((channels, TAPS), jnp.float32), strain], axis=1)
    decimated = decimate(extended, fir_weights(fir_taps, offset), TD)
    all_rows = jnp.arange(TD, dtype=jnp.int32)
    white_all = whiten(spectrum_block(all_rows, all_rows, decimated))
    source_ids = jnp.arange(NV, dtype=jnp.int32) // SRC_DEV * CH_DEV + source_channel
    chosen = jnp.take(white_all, source_ids, axis=1).T
    chosen = chosen.reshape(NBLK, SRC_DEV, TD).transpose(1, 0, 2).reshape(NV, TD)
    table = lag_table(all_rows, 0)
    width_block = math.gcd(CH, 128)
    receiver_blocks = white_all.reshape(TD, CH // width_block, width_block).transpose(1, 0, 2)
    source_block = math.gcd(NV, 32)
    grouped = chosen.reshape(NV // source_block, source_block, TD)
    norm_scale = FREQ ** (-0.5)

    def per_receivers(receivers):

        def per_sources(sources):
            cross = cross_block(sources, receivers)
            return jnp.einsum('bfc,ft->bct', cross.astype(jnp.float32), table.astype(jnp.float32), precision=lax.Precision.HIGHEST)
        summed = lax.map(per_sources, grouped).reshape(NV, width_block, LAGS)
        return (summed * norm_scale).astype(jnp.bfloat16)
    stacked = lax.map(per_receivers, receiver_blocks)
    return stacked.transpose(1, 0, 2, 3).reshape(SRC_DEV, NBLK, CH, LAGS)
```

```python
import functools

import jax
import jax.numpy as jnp
import ml_dtypes
import numpy as np
from jax import lax
from jax.experimental import pallas as pl
from jax.experimental.pallas import tpu as pltpu
from jax.sharding import PartitionSpec as P

TD = 2048
HALF = 1024
TAPS = 64
CH = 128
NA = 16
NB = 8
SHAPE = (4, 4, 4, 2)
NN = (((1,), (0,)), ((), ()))
NT = (((1,), (1,)), ((), ()))
F32 = jnp.float32
BF16 = jnp.bfloat16


def bins(odd):
    col = np.arange(512)
    rank = col // 128 * 8 + col % 128 // 16
    return 64 * (col % 16) + 2 * rank + odd


def split_table(table):
    high = table.astype(ml_dtypes.bfloat16)
    low = (table - high.astype(np.float64)).astype(ml_dtypes.bfloat16)
    return np.stack([high, low])


def cot(num):
    return 1.0 / np.tan(np.pi * num / TD)


@functools.cache
def tables():
    even, odd = bins(0), bins(1)
    time = np.arange(HALF)[:, None]

    def wave(freq, times):
        ang = 2 * np.pi * (freq[None, :] * times % TD) / TD
        return np.cos(ang), -np.sin(ang)

    re, im = wave(even, time)
    nyquist = (-1.0) ** np.arange(HALF)
    im = im.copy()
    im[:, 0] = nyquist
    dft = np.concatenate([re, im], 1)
    fe, fo = even[:, None], odd[None, :]
    mix = np.zeros((HALF, HALF))
    norm = np.where(even == 0, 1.0 / HALF, 2.0 / HALF)[:, None]
    mix[:512, :512] = norm
    mix[:512, 512:] = -0.5 * (cot(fe + fo) + cot(fo - fe)) * norm
    mix[512:, :512] = -0.5 * (cot(fe + fo) + cot(fe - fo)) * norm
    mix[512, :512] = 1.0 / HALF
    mix[512, 512:] = (-0.5 * (cot(HALF + fo) + cot(fo - HALF)) / HALF)[0]
    tail = np.zeros((128, TD))
    rows = np.arange(16)[:, None]
    tail[:16] = np.concatenate(wave(even, rows) + tuple(-w for w in wave(odd, rows)), 1)
    both = np.concatenate([even, odd])[None, :]
    shift = 2 * np.pi * (both * np.arange(NB)[:, None] % TD) / TD
    coarse = 2 * np.pi * (both * (NB * np.arange(NA)[:, None] - 64) % TD) / TD
    place = np.zeros((TAPS, 640), np.float32)
    place[np.arange(TAPS), 128 - np.arange(TAPS)] = 1.0
    return dict(
        dft=split_table(dft),
        mix=split_table(mix),
        tail=split_table(tail),
        shift=np.stack([np.cos(shift), np.sin(shift)]).astype(np.float32),
        coarse=(np.stack([np.cos(coarse), np.sin(coarse)]) / 32.0).astype(np.float32),
        place=place,
    )


def split(values):
    high = values.astype(BF16)
    return high, (values - high.astype(F32)).astype(BF16)


def dot3(left, right, dims=NN):
    (lh, ll), (rh, rl) = left, right
    dot = functools.partial(lax.dot_general, dimension_numbers=dims, preferred_element_type=F32)
    return dot(lh, rh) + (dot(ll, rh) + dot(lh, rl))


def prepare_kernel(
    place_idx, strain, offset, fir, place, dft, e32, e16, tail_out, own_msg, far_msg, ext, dec
):
    sec = place_idx[0]
    width = ext.shape[1]
    ext[:, :128] = jnp.zeros((CH, 128), F32)
    ext[:, width - 128 :] = jnp.zeros((CH, 128), F32)
    ext[:, 128 : width - 128] = strain[...]
    taps = jnp.broadcast_to(fir[...], (8, TAPS))
    row = lax.dot_general(
        taps, place[...], NN, precision=lax.Precision.HIGHEST, preferred_element_type=F32
    )
    band = pltpu.roll(jnp.broadcast_to(row[:1], (128, 640)), 0, 1, stride=4, stride_axis=0)
    band = split(band)
    off = offset[...]
    raw = ext[...]
    shifted = raw
    for step in range(1, 4):
        shifted = jnp.where(off == step, pltpu.roll(raw, width - step, 1), shifted)
    high, low = split(shifted)
    for block in range(8):
        at = slice(512 * block, 512 * block + 640)
        dec[:, 128 * block : 128 * block + 128] = dot3((high[:, at], low[:, at]), band, NT)
    at = slice(4096, 4352)
    seam = dot3((high[:, at], low[:, at]), (band[0][:, :256], band[1][:, :256]), NT)
    seam = jnp.where(sec == 0, seam, 0.0)
    tail_out[...] = seam
    even = dot3(split(dec[...]), (dft[0], dft[1]))
    e32[...] = even
    e16[...] = even.astype(BF16)
    for slot, msg in ((sec, own_msg), (1 - sec, far_msg)):
        src = place_idx[1 + slot]
        values = e32[pl.ds(src, 1), :]
        for part in range(8):
            msg[part : part + 1, :] = values[:, 128 * part : 128 * part + 128]
        msg[8:9, :] = tail_out[pl.ds(src, 1), :]
        msg[9:16, :] = jnp.zeros((7, 128), F32)
    far_msg[16:32, :] = seam.T[:16]


def whole_window(own, far, seam, sign, mix, tail):
    even = own + far
    odd = dot3(split((own - far) * sign), mix)
    added = dot3(split(seam), tail)
    even = even + added[:, :HALF]
    odd = odd + added[:, HALF:]
    column = lax.broadcasted_iota(jnp.int32, even.shape, 1)
    even = jnp.where(column == 512, 0.0, even)
    spectrum = jnp.concatenate([even, odd], 1)
    power = jnp.zeros((own.shape[0], 128), F32)
    for part in range(16):
        piece = spectrum[:, 128 * part : 128 * part + 128]
        power = power + piece * piece
    for step in (16, 32, 64):
        power = power + pltpu.roll(power, step, 1)
    factor = 1.0 / jnp.sqrt(power * (1.0 / 128.0) + 1e-06)
    return spectrum * jnp.concatenate([factor] * 16, 1)


def source_kernel(place_idx, own, far, mix, tail, out):
    sec = place_idx[0]
    sign = jnp.where(sec == 0, 1.0, -1.0).astype(F32)

    def line(ref):
        return jnp.concatenate([ref[part : part + 1, :] for part in range(8)], 1)

    def rows(values):
        return jnp.broadcast_to(values, (8, values.shape[1]))

    seam = jnp.where(sec == 0, own[8:9, :], far[8:9, :])
    white = whole_window(
        rows(line(own)), rows(line(far)), rows(seam), sign, (mix[0], mix[1]), (tail[0], tail[1])
    )
    parts = [white[:1, 128 * part : 128 * part + 128] for part in range(16)]
    out[...] = jnp.concatenate(parts, 0).astype(BF16)


def receiver_kernel(place_idx, own, far, own_tail, far_tail, mix, tail, coarse, out):
    sec = place_idx[0]
    sign = jnp.where(sec == 0, 1.0, -1.0).astype(F32)
    seam = jnp.where(sec == 0, own_tail[...], far_tail[...])
    white = whole_window(
        own[...], far[...].astype(F32), seam, sign, (mix[0], mix[1]), (tail[0], tail[1])
    )

    def lag(a, carry):
        for half in (0, 1):
            at = HALF * half
            re = white[:, at : at + 512]
            im = white[:, at + 512 : at + HALF]
            cos = coarse[0, pl.ds(a, 1), 512 * half : 512 * half + 512]
            sin = coarse[1, pl.ds(a, 1), 512 * half : 512 * half + 512]
            out[a, :, at : at + 512] = (re * cos - im * sin).astype(BF16)
            out[a, :, at + 512 : at + HALF] = (re * sin + im * cos).astype(BF16)
        return carry

    lax.fori_loop(0, NA, lag, 0)


def correlate_kernel(place_idx, chosen, turned, shift, out, left, sums):
    step = pl.program_id(0)

    @pl.when(step == 0)
    def _():
        def pair(two, carry):
            parts = [chosen[2 * two + k].astype(F32) for k in range(2)]
            at = pl.ds(pl.multiple_of(16 * two, 16), 16)
            for half in (0, 1):
                for part in range(4):
                    row = 8 * half + part
                    lane = 512 * half + 128 * part
                    cos = shift[0, :, lane : lane + 128]
                    sin = shift[1, :, lane : lane + 128]
                    re = [jnp.broadcast_to(p[row : row + 1], (NB, 128)) for p in parts]
                    im = [jnp.broadcast_to(p[row + 4 : row + 5], (NB, 128)) for p in parts]
                    col = 1024 * half + 128 * part
                    left[at, col : col + 128] = jnp.concatenate(
                        [re[k] * cos + im[k] * sin for k in range(2)], 0
                    ).astype(BF16)
                    left[at, col + 512 : col + 640] = jnp.concatenate(
                        [im[k] * cos - re[k] * sin for k in range(2)], 0
                    ).astype(BF16)
            return carry

        lax.fori_loop(0, 64, pair, 0)

    width = turned.shape[0]
    total = lax.dot_general(
        left[...], turned[...].reshape(width * CH, TD), NT, preferred_element_type=F32
    )
    for k in range(width):
        sums[step * width + k] = total[:, CH * k : CH * k + CH]

    @pl.when(step == pl.num_programs(0) - 1)
    def _():
        y, z, x, core = (place_idx[k] for k in range(4))

        def finish(rel, carry):
            dc, dx, dy, dz = rel // 64, rel // 16 % 4, rel // 4 % 4, rel % 4
            block = (
                (lax.rem(y - dy + 4, 4) * 4 + lax.rem(z - dz + 4, 4)) * 4 + lax.rem(x - dx + 4, 4)
            ) * 2 + lax.rem(core + dc, 2)
            at = pl.ds(pl.multiple_of(rel * NB, NB), NB)
            tile = sums[:, at, :].reshape(NA * NB, CH)
            out[block] = tile.T.astype(BF16)
            return carry

        lax.fori_loop(0, 128, finish, 0, unroll=4)


def vmem(count):
    return [pl.BlockSpec(memory_space=pltpu.VMEM)] * count


SMEM = pl.BlockSpec(memory_space=pltpu.SMEM)
LIMIT = pltpu.CompilerParams(vmem_limit_bytes=56 * 2**20)


def prepare(place_idx, strain, offset, fir, tab):
    width = strain.shape[1] + 256
    shapes = [((CH, HALF), F32), ((CH, HALF), BF16), ((CH, 128), F32), ((16, 128), F32), ((32, 128), F32)]
    return pl.pallas_call(
        prepare_kernel,
        out_shape=[jax.ShapeDtypeStruct(*s) for s in shapes],
        in_specs=[SMEM] + vmem(5),
        out_specs=vmem(5),
        scratch_shapes=[pltpu.VMEM((CH, width), F32), pltpu.VMEM((CH, HALF), F32)],
        compiler_params=LIMIT,
        name="prepare",
    )(place_idx, strain, offset, fir, tab["place"], tab["dft"])


def finish_sources(place_idx, own, far, tab):
    return pl.pallas_call(
        source_kernel,
        out_shape=jax.ShapeDtypeStruct((16, 128), BF16),
        in_specs=[SMEM] + vmem(4),
        out_specs=vmem(1)[0],
        compiler_params=LIMIT,
        name="finish_sources",
    )(place_idx, own, far, tab["mix"], tab["tail"])


def turn_receivers(place_idx, own, far, own_tail, far_tail, tab):
    rows = 32

    def whole(*shape):
        return pl.BlockSpec(shape, lambda c: (0,) * len(shape))

    def part(*shape):
        return pl.BlockSpec(shape, lambda c: (c, 0))

    return pl.pallas_call(
        receiver_kernel,
        grid=(CH // rows,),
        out_shape=jax.ShapeDtypeStruct((NA, CH, TD), BF16),
        in_specs=[
            SMEM,
            part(rows, HALF),
            part(rows, HALF),
            part(rows, 128),
            part(rows, 128),
            whole(2, HALF, HALF),
            whole(2, 128, TD),
            whole(2, NA, HALF),
        ],
        out_specs=pl.BlockSpec((NA, rows, TD), lambda c: (0, c, 0)),
        compiler_params=LIMIT,
        cost_estimate=pl.CostEstimate(flops=3 * 2 * 128 * 1024 * 1024, bytes_accessed=16 * 2**20, transcendentals=0),
        name="turn_receivers",
    )(place_idx, own, far, own_tail, far_tail, tab["mix"], tab["tail"], tab["coarse"])


def correlate(where, chosen, turned, tab):
    width = 4
    return pl.pallas_call(
        correlate_kernel,
        grid=(NA // width,),
        out_shape=jax.ShapeDtypeStruct((128, CH, 128), BF16),
        in_specs=[
            SMEM,
            pl.BlockSpec((128, 16, 128), lambda n: (0, 0, 0)),
            pl.BlockSpec((width, CH, TD), lambda n: (n, 0, 0)),
            pl.BlockSpec((2, NB, HALF), lambda n: (0, 0, 0)),
        ],
        out_specs=pl.BlockSpec((128, CH, 128), lambda n: (0, 0, 0)),
        scratch_shapes=[pltpu.VMEM((128 * NB, TD), BF16), pltpu.VMEM((NA, 128 * NB, CH), F32)],
        compiler_params=LIMIT,
        cost_estimate=pl.CostEstimate(flops=2 * 2**32, bytes_accessed=13 * 2**20, transcendentals=0),
        name="correlate",
    )(where, chosen, turned, tab["shift"])


def coordinates(index):
    y, z, x, core = SHAPE
    return [index // (z * x * core), index // (x * core) % z, index // core % x, index % core]


def around(values, dim, by):
    def target(index):
        at = coordinates(index)
        at[dim] = (at[dim] + by) % SHAPE[dim]
        return ((at[0] * SHAPE[1] + at[1]) * SHAPE[2] + at[2]) * SHAPE[3] + at[3]

    return lax.ppermute(values, "rcv", [(i, target(i)) for i in range(int(np.prod(SHAPE)))])


def gather(values):
    values = values[None]
    for dim in (1, 0, 2, 3):
        values = jnp.concatenate(
            [values] + [around(values, dim, by) for by in range(1, SHAPE[dim])], 0
        )
    return values


def per_device(strain, offset, fir_taps, source_channel):
    tab = tables()
    sec = lax.axis_index("sec").astype(jnp.int32)
    rcv = lax.axis_index("rcv").astype(jnp.int32)
    place_idx = jnp.concatenate([sec[None], source_channel.astype(jnp.int32)])
    where = jnp.stack(coordinates(rcv))
    e32, e16, own_tail, own_msg, far_msg = prepare(
        place_idx, strain, offset[:, None], fir_taps[None, :], tab
    )
    swap = [(0, 1), (1, 0)]
    got_msg = lax.ppermute(far_msg, "sec", swap)
    got16 = lax.ppermute(e16, "sec", swap)
    chosen = gather(finish_sources(place_idx, own_msg, got_msg[:16], tab))
    far_tail = jnp.pad(got_msg[16:].T, ((0, 0), (0, 112)))
    turned = turn_receivers(place_idx, e32, got16, own_tail, far_tail, tab)
    return correlate(where, chosen, turned, tab)[None]


def solution(mesh):
    in_specs = (P("rcv", "sec"), P("rcv"), P(), P("rcv"))
    out_specs = P("sec", None, "rcv", None)
    return jax.shard_map(
        per_device, mesh=mesh, in_specs=in_specs, out_specs=out_specs, check_vma=False
    )
```

```python
import functools

import jax
import jax.numpy as jnp
import ml_dtypes
import numpy as np
from jax import lax
from jax.experimental import pallas as pl
from jax.experimental.pallas import tpu as pltpu
from jax.sharding import PartitionSpec as P

TD = 2048
HALF = 1024
TAPS = 64
CH = 128
NA = 16
NB = 8
SHAPE = (4, 4, 4, 2)
NN = (((1,), (0,)), ((), ()))
NT = (((1,), (1,)), ((), ()))
F32 = jnp.float32
BF16 = jnp.bfloat16


def bins(first, step, count):
    col = np.arange(count)
    rank = col // 128 * 8 + col % 128 // 16
    return 64 * (col % 16) + step * rank + first


def split_table(table):
    high = table.astype(ml_dtypes.bfloat16)
    low = (table - high.astype(np.float64)).astype(ml_dtypes.bfloat16)
    return np.stack([high, low])


def cot(num):
    return 1.0 / np.tan(np.pi * num / TD)


def wave(freq, times):
    ang = 2 * np.pi * (freq[None, :] * times % TD) / TD
    return np.cos(ang), -np.sin(ang)


@functools.cache
def tables():
    quads = [bins(0, 4, 256), bins(2, 4, 256)]
    odd = bins(1, 2, 512)
    even = np.concatenate(quads)
    time = np.arange(512)[:, None]
    dft = []
    for freq in quads:
        re, im = wave(freq, time)
        if freq[0] == 0:
            im[:, 0] = (-1.0) ** np.arange(512)
        dft.append(split_table(np.concatenate([re, im], 1)))
    fe, fo = even[:, None], odd[None, :]
    norm = 2.0 / HALF
    re_im = -0.5 * (cot(fe + fo) + cot(fo - fe)) * np.where(fe == 0, 0.5 * norm, norm)
    im_re = -0.5 * (cot(fe + fo) + cot(fe - fo)) * np.where(fe == 0, 0.0, norm)
    nyquist = -0.5 * (cot(HALF + fo) + cot(fo - HALF)) / HALF
    rows = np.arange(16)[:, None]
    tail = np.concatenate(
        wave(quads[0], rows) + wave(quads[1], rows) + tuple(-w for w in wave(odd, rows)), 1
    )
    both = np.concatenate([even, odd])[None, :]
    shift = 2 * np.pi * (both * np.arange(NB)[:, None] % TD) / TD
    coarse = 2 * np.pi * (both * (NB * np.arange(NA)[:, None] - 64) % TD) / TD
    place = np.zeros((TAPS, 640), np.float32)
    place[np.arange(TAPS), 128 - np.arange(TAPS)] = 1.0
    return dict(
        dft=np.stack(dft),
        mix=np.stack([split_table(re_im), split_table(im_re)]),
        nyquist=nyquist.astype(np.float32),
        tail=split_table(tail),
        shift=np.stack([np.cos(shift), np.sin(shift)]).astype(np.float32),
        coarse=(np.stack([np.cos(coarse), np.sin(coarse)], 1) / 32.0).astype(np.float32),
        place=place,
    )


PAIRS = [(128 * k, at, at + 256) for k, at in enumerate((0, 128, 512, 640))]
ODD_PAIRS = [(512 + 128 * k, 1024 + 128 * k, 1536 + 128 * k) for k in range(4)]
ALL_PAIRS = PAIRS + ODD_PAIRS


def split(values):
    high = values.astype(BF16)
    return high, (values - high.astype(F32)).astype(BF16)


def dot3(values, table, dims=NN):
    high, low = split(values) if not isinstance(values, tuple) else values
    dot = functools.partial(lax.dot_general, dimension_numbers=dims, preferred_element_type=F32)
    rows = high.shape[0]
    both = dot(jnp.concatenate([high, low], 0), table[0])
    return both[:rows] + (both[rows:] + dot(high, table[1]))


def filter_band(fir, place):
    taps = jnp.broadcast_to(fir, (8, TAPS))
    row = lax.dot_general(
        taps, place, NN, precision=lax.Precision.HIGHEST, preferred_element_type=F32
    )
    band = pltpu.roll(jnp.broadcast_to(row[:1], (128, 640)), 0, 1, stride=4, stride_axis=0)
    return split(band)


def decimate(ext, off, band, dec):
    width = ext.shape[1]
    raw = ext[...]
    shifted = raw
    for step in range(1, 4):
        shifted = jnp.where(off == step, pltpu.roll(raw, width - step, 1), shifted)
    high, low = split(shifted)
    for block in range(8):
        at = slice(512 * block, 512 * block + 640)
        dec[:, 128 * block : 128 * block + 128] = dot3((high[:, at], low[:, at]), band, NT)
    at = slice(4096, 4352)
    seam = dot3((high[:, at], low[:, at]), (band[0][:, :256], band[1][:, :256]), NT)
    return jnp.where(lax.axis_index("sec") == 0, seam, 0.0)


def even_bins(dec, dft, out):
    first, second = dec[:, :512], dec[:, 512:]
    for quad, folded in enumerate((first + second, first - second)):
        out[:, 512 * quad : 512 * quad + 512] = dot3(folded, (dft[quad, 0], dft[quad, 1]))


def pad_edges(ext):
    width = ext.shape[1]
    ext[:, :128] = jnp.zeros((ext.shape[0], 128), F32)
    ext[:, width - 128 :] = jnp.zeros((ext.shape[0], 128), F32)


def own_sources_kernel(
    source, offsets, strain, fir, place, dft_hbm, msg, near, ext, dec, even, dft, sems
):
    copies = []
    for slot in range(2):
        group = pl.multiple_of(source[slot] // 8 * 8, 8)
        copies.append(pltpu.make_async_copy(strain.at[pl.ds(group, 8)], near.at[slot], sems.at[slot]))
    fetch = pltpu.make_async_copy(dft_hbm, dft, sems.at[2])
    for copy in copies:
        copy.start()
    fetch.start()
    ext[...] = jnp.zeros(ext.shape, F32)
    band = filter_band(fir[...], place[...])
    row_id = lax.broadcasted_iota(jnp.int32, (8, 1), 0)
    off = jnp.where(row_id == 0, offsets[source[0]], offsets[source[1]])
    width = ext.shape[1]
    for slot in range(2):
        copies[slot].wait()
        ext[slot : slot + 1, 128 : width - 128] = near[slot, pl.ds(source[slot] % 8, 1), :]
    seam = decimate(ext, off, band, dec)
    fetch.wait()
    even_bins(dec, dft, even)
    for slot in range(2):
        values = even[slot : slot + 1, :]
        rows = [values[:, 128 * part : 128 * part + 128] for part in range(8)]
        rows += [seam[slot : slot + 1], jnp.zeros((7, 128), F32)]
        block = jnp.concatenate(rows, 0)
        for z in range(msg.shape[0] // 2):
            msg[msg.shape[0] // 2 * slot + z] = block


def prepare_kernel(
    strain, offset, fir, place, dft_hbm, e32_hbm, e16, tail_out, ext, dec, e32, dft, sems
):
    width = ext.shape[1]
    load = pltpu.make_async_copy(strain, ext.at[:, 128 : width - 128], sems.at[0])
    fetch = pltpu.make_async_copy(dft_hbm, dft, sems.at[1])
    load.start()
    fetch.start()
    pad_edges(ext)
    band = filter_band(fir[...], place[...])
    off = jnp.broadcast_to(offset[...].astype(F32), (CH, CH)).T[:, :1]
    load.wait()
    seam = decimate(ext, off, band, dec)
    tail_out[...] = seam
    fetch.wait()
    even_bins(dec, dft, e32)
    keep = pltpu.make_async_copy(e32, e32_hbm, sems.at[0])
    keep.start()
    for part in range(8):
        at = slice(128 * part, 128 * part + 128)
        e16[at, :] = e32[:, at].astype(BF16)
    e16[HALF : HALF + 16, :] = seam.T[:16].astype(BF16)
    keep.wait()


def whole_window(first, second, seam, mix, nyquist, tail):
    even = first + second
    diff = first - second
    real = jnp.concatenate([diff[:, :256], diff[:, 512:768]], 1)
    imag = jnp.concatenate([diff[:, 256:512], diff[:, 768:]], 1)
    added = dot3(seam[:, :16], (tail[0], tail[1]))
    even = even + added[:, :HALF]
    column = lax.broadcasted_iota(jnp.int32, even.shape, 1)
    even = jnp.where(column == 256, 0.0, even)
    ends = jnp.where(
        lax.broadcasted_iota(jnp.int32, (diff.shape[0], 128), 1) == 0,
        imag[:, :128] - real[:, :128],
        0.0,
    )
    total = ends
    for part in range(4):
        total = total + 2.0 * real[:, 128 * part : 128 * part + 128]
    start = jnp.sum(total, axis=1, keepdims=True) * (1.0 / HALF)
    odd_im = dot3(real, (mix[0, 0], mix[0, 1])) + imag[:, :1] * nyquist[...]
    odd_re = dot3(imag, (mix[1, 0], mix[1, 1])) + start
    spectrum = jnp.concatenate(
        [even, odd_re + added[:, HALF : HALF + 512], odd_im + added[:, HALF + 512 :]], 1
    )
    power = jnp.zeros((diff.shape[0], 128), F32)
    for part in range(16):
        piece = spectrum[:, 128 * part : 128 * part + 128]
        power = power + piece * piece
    for step in (16, 32, 64):
        power = power + pltpu.roll(power, step, 1)
    factor = 1.0 / jnp.sqrt(power * (1.0 / 128.0) + 1e-06)
    return spectrum * jnp.concatenate([factor] * 16, 1)


def source_kernel(parts, mix, nyquist, tail, out):
    def lines(half):
        rows = [parts[4 * half : 4 * half + 4, part, :] for part in range(8)]
        both = jnp.concatenate(rows, 1)
        return jnp.concatenate([both, both], 0)

    seam = parts[0:4, 8, :]
    white = whole_window(
        lines(0), lines(1), jnp.concatenate([seam, seam], 0), mix, nyquist, tail
    )
    rows = [
        white[k : k + 1, 128 * part : 128 * part + 128] for k in range(4) for part in range(16)
    ]
    block = jnp.concatenate(rows, 0).astype(BF16)
    for peer in range(out.shape[0]):
        out[peer] = block


def receiver_kernel(own_hbm, far, own_tail, mix, nyquist, tail, white, own, sem):
    load = pltpu.make_async_copy(own_hbm, own, sem)
    load.start()
    first_sec = lax.axis_index("sec") == 0
    got = jnp.concatenate(
        [far[128 * part : 128 * part + 128, :].astype(F32) for part in range(8)], 1
    )
    got_seam = jnp.concatenate(
        [far[HALF : HALF + 16, :].astype(F32), jnp.zeros((112, 128), F32)], 0
    ).T
    load.wait()
    mine = own[...]
    white[...] = whole_window(
        jnp.where(first_sec, mine, got),
        jnp.where(first_sec, got, mine),
        jnp.where(first_sec, own_tail[...], got_seam),
        mix,
        nyquist,
        tail,
    )


LINES = ((0, 64), (64, 64))
PART = 8
CHUNKS = NA // PART
SEND = 32


def turn_sources(chosen, shift, left, first, count, row):
    for two in range(count // 2):
        parts = [chosen[first + 2 * two + k].astype(F32) for k in range(2)]
        at = slice(row + 16 * two, row + 16 * two + 16)
        for col, re_at, im_at in ALL_PAIRS:
            cos = shift[0, :, col : col + 128]
            sin = shift[1, :, col : col + 128]
            up, low = re_at // 128, im_at // 128
            re = [jnp.broadcast_to(p[up : up + 1], (NB, 128)) for p in parts]
            im = [jnp.broadcast_to(p[low : low + 1], (NB, 128)) for p in parts]
            left[at, re_at : re_at + 128] = jnp.concatenate(
                [re[k] * cos + im[k] * sin for k in range(2)], 0
            ).astype(BF16)
            left[at, im_at : im_at + 128] = jnp.concatenate(
                [im[k] * cos - re[k] * sin for k in range(2)], 0
            ).astype(BF16)


def correlate_kernel(chosen, white, shift, coarse, out_hbm, *scratch):
    turned, rest = scratch[:CHUNKS], scratch[CHUNKS:]
    left, sums, (out, sems) = rest[:2], rest[2:4], rest[4:]

    def share(line, n):
        first, count = LINES[line]
        each = count // CHUNKS
        return first, n * each, each

    def turn(line, n):
        if line < len(LINES):
            first, at, count = share(line, n)
            turn_sources(chosen, shift, left[line % 2], first + at, count, at * NB)

    def build(n):
        if n >= CHUNKS:
            return
        for k in range(PART):
            a = n * PART + k
            at = slice(k * CH, k * CH + CH)
            for col, re_at, im_at in ALL_PAIRS:
                re = white[:, re_at : re_at + 128]
                im = white[:, im_at : im_at + 128]
                cos = coarse[a, 0:1, col : col + 128]
                sin = coarse[a, 1:2, col : col + 128]
                turned[n][at, re_at : re_at + 128] = (re * cos - im * sin).astype(BF16)
                turned[n][at, im_at : im_at + 128] = (re * sin + im * cos).astype(BF16)

    def product(line, n):
        rows = LINES[line][1] * NB
        total = lax.dot_general(
            left[line % 2][:rows], turned[n][...], NT, preferred_element_type=F32
        )
        for k in range(PART):
            sums[line % 2][n * PART + k, :rows] = total[:, CH * k : CH * k + CH]

    def finish(line, n):
        if line < 0:
            return
        first, start, count = share(line, n)
        for k in range(start, start + count):
            rel = first + k
            tile = sums[line % 2][:, k * NB : k * NB + NB, :].reshape(NA * NB, CH)
            out[rel // 32 * 32 + rel % 4 * 8 + rel % 32 // 4] = tile.T.astype(BF16)
            if (rel + 1) % SEND == 0:
                send(rel // SEND).start()

    def send(group):
        at = pl.ds(group * SEND, SEND)
        return pltpu.make_async_copy(out.at[at], out_hbm.at[at], sems.at[group])

    build(0)
    for n in range(CHUNKS):
        turn(0, n)
    for line in range(len(LINES)):
        for n in range(CHUNKS):
            product(line, n)
            if line == 0:
                build(n + 1)
            turn(line + 1, n)
            finish(line - 1, n)
    for n in range(CHUNKS):
        finish(len(LINES) - 1, n)
    for group in range(128 // SEND):
        send(group).wait()


def vmem(count):
    return [pl.BlockSpec(memory_space=pltpu.VMEM)] * count


SMEM = pl.BlockSpec(memory_space=pltpu.SMEM)
HBM = pl.BlockSpec(memory_space=pltpu.HBM)


def limit(mib):
    return pltpu.CompilerParams(vmem_limit_bytes=mib * 2**20)


def cost(mega_flops, mib):
    return pl.CostEstimate(flops=mega_flops * 10**6, bytes_accessed=mib * 2**20, transcendentals=0)


def own_sources(source, offset, strain, fir, tab):
    width = strain.shape[1] + 256
    return pl.pallas_call(
        own_sources_kernel,
        out_shape=jax.ShapeDtypeStruct((8, 16, 128), F32),
        in_specs=[SMEM, SMEM, HBM] + vmem(2) + [HBM],
        out_specs=vmem(1)[0],
        scratch_shapes=[
            pltpu.VMEM((2, 8, strain.shape[1]), F32),
            pltpu.VMEM((8, width), F32),
            pltpu.VMEM((8, HALF), F32),
            pltpu.VMEM((8, HALF), F32),
            pltpu.VMEM((2, 2, 512, 512), BF16),
            pltpu.SemaphoreType.DMA((3,)),
        ],
        compiler_params=limit(62),
        cost_estimate=cost(500, 3),
        name="own_sources",
    )(source, offset, strain, fir, tab["place"], tab["dft"])


def prepare(strain, offset, fir, tab):
    width = strain.shape[1] + 256
    shapes = [((CH, HALF), F32), ((HALF + 16, 128), BF16), ((CH, 128), F32)]
    return pl.pallas_call(
        prepare_kernel,
        out_shape=[jax.ShapeDtypeStruct(*s) for s in shapes],
        in_specs=[HBM] + vmem(3) + [HBM],
        out_specs=[HBM] + vmem(2),
        scratch_shapes=[
            pltpu.VMEM((CH, width), F32),
            pltpu.VMEM((CH, HALF), F32),
            pltpu.VMEM((CH, HALF), F32),
            pltpu.VMEM((2, 2, 512, 512), BF16),
            pltpu.SemaphoreType.DMA((2,)),
        ],
        compiler_params=limit(62),
        cost_estimate=cost(4000, 6),
        name="prepare",
    )(strain, offset, fir, tab["place"], tab["dft"])


def finish_sources(parts, peers, tab):
    return pl.pallas_call(
        source_kernel,
        out_shape=jax.ShapeDtypeStruct((peers, 64, 128), BF16),
        in_specs=vmem(4),
        out_specs=vmem(1)[0],
        compiler_params=limit(32),
        cost_estimate=cost(500, 3),
        name="finish_sources",
    )(parts, tab["mix"], tab["nyquist"], tab["tail"])


def finish_receivers(own, far, own_tail, tab):
    return pl.pallas_call(
        receiver_kernel,
        out_shape=jax.ShapeDtypeStruct((CH, TD), F32),
        in_specs=[HBM] + vmem(5),
        out_specs=vmem(1)[0],
        scratch_shapes=[pltpu.VMEM((CH, HALF), F32), pltpu.SemaphoreType.DMA],
        compiler_params=limit(32),
        cost_estimate=cost(3000, 6),
        name="finish_receivers",
    )(own, far, own_tail, tab["mix"], tab["nyquist"], tab["tail"])


def correlate(chosen, white, tab):
    longest = max(count for _, count in LINES)
    return pl.pallas_call(
        correlate_kernel,
        out_shape=jax.ShapeDtypeStruct((128, CH, 128), BF16),
        in_specs=vmem(4),
        out_specs=HBM,
        scratch_shapes=[pltpu.VMEM((PART * CH, TD), BF16)] * CHUNKS
        + [pltpu.VMEM((longest * NB, TD), BF16)] * 2
        + [pltpu.VMEM((NA, longest * NB, CH), F32)] * 2
        + [pltpu.VMEM((128, CH, 128), BF16), pltpu.SemaphoreType.DMA((128 // SEND,))],
        compiler_params=limit(44),
        cost_estimate=cost(9000, 13),
        name="correlate",
    )(chosen, white, tab["shift"], tab["coarse"])


def section_groups(size):
    y, z, x, core = SHAPE
    plane = x * core
    return [
        [s * size + (j * z + k) * plane + i for s in range(2) for k in range(z)]
        for j in range(y)
        for i in range(plane)
    ]


def plane_groups():
    y, z, x, core = SHAPE
    plane = x * core
    return [[(j * z + k) * plane + i for j in range(y) for i in range(plane)] for k in range(z)]


def per_device(strain, offset, fir_taps, source_channel):
    tab = tables()
    msg = own_sources(source_channel, offset, strain, fir_taps[None, :], tab)
    parts = lax.all_to_all(
        msg, ("sec", "rcv"), 0, 0, axis_index_groups=section_groups(lax.axis_size("rcv"))
    )
    strain, msg = lax.optimization_barrier((strain, msg))
    e32, e16, own_tail = prepare(strain, offset[None, :], fir_taps[None, :], tab)
    got16 = lax.ppermute(e16, "sec", [(0, 1), (1, 0)])
    groups = plane_groups()
    mine = finish_sources(parts, len(groups[0]), tab)
    chosen = lax.all_to_all(mine, "rcv", 0, 0, axis_index_groups=groups)
    white = finish_receivers(e32, got16, own_tail, tab)
    return correlate(chosen.reshape(128, 16, 128), white, tab)[None]


def solution(mesh):
    in_specs = (P("rcv", "sec"), P("rcv"), P(), P("rcv"))
    out_specs = P("sec", None, "rcv", None)
    return jax.shard_map(
        per_device, mesh=mesh, in_specs=in_specs, out_specs=out_specs, check_vma=False
    )
```

```python
import functools

import jax
import jax.numpy as jnp
import ml_dtypes
import numpy as np
from jax import lax
from jax.experimental import pallas as pl
from jax.experimental.pallas import tpu as pltpu
from jax.sharding import PartitionSpec as P

TD = 2048
HALF = 1024
TAPS = 64
CH = 128
NA = 16
NB = 8
SHAPE = (4, 4, 4, 2)
NN = (((1,), (0,)), ((), ()))
NT = (((1,), (1,)), ((), ()))
F32 = jnp.float32
BF16 = jnp.bfloat16


def bins(first, step, count):
    col = np.arange(count)
    rank = col // 128 * 8 + col % 128 // 16
    return 64 * (col % 16) + step * rank + first


def split_table(table):
    high = table.astype(ml_dtypes.bfloat16)
    low = (table - high.astype(np.float64)).astype(ml_dtypes.bfloat16)
    return np.stack([high, low])


def cot(num):
    return 1.0 / np.tan(np.pi * num / TD)


def wave(freq, times):
    ang = 2 * np.pi * (freq[None, :] * times % TD) / TD
    return np.cos(ang), -np.sin(ang)


@functools.cache
def tables():
    quads = [bins(0, 4, 256), bins(2, 4, 256)]
    odd = bins(1, 2, 512)
    even = np.concatenate(quads)
    time = np.arange(512)[:, None]
    dft = []
    for freq in quads:
        re, im = wave(freq, time)
        if freq[0] == 0:
            im[:, 0] = (-1.0) ** np.arange(512)
        dft.append(split_table(np.concatenate([re, im], 1)))
    fe, fo = even[:, None], odd[None, :]
    norm = 2.0 / HALF
    re_im = -0.5 * (cot(fe + fo) + cot(fo - fe)) * np.where(fe == 0, 0.5 * norm, norm)
    im_re = -0.5 * (cot(fe + fo) + cot(fe - fo)) * np.where(fe == 0, 0.0, norm)
    nyquist = -0.5 * (cot(HALF + fo) + cot(fo - HALF)) / HALF
    rows = np.arange(16)[:, None]
    tail = np.concatenate(
        wave(quads[0], rows) + wave(quads[1], rows) + tuple(-w for w in wave(odd, rows)), 1
    )
    both = np.concatenate([even, odd])[None, :]
    shift = 2 * np.pi * (both * np.arange(NB)[:, None] % TD) / TD
    coarse = 2 * np.pi * (both * (NB * np.arange(NA)[:, None] - 64) % TD) / TD
    return dict(
        dft=np.stack(dft),
        mix=np.stack([split_table(re_im), split_table(im_re)]),
        nyquist=nyquist.astype(np.float32),
        tail=split_table(tail),
        shift=np.stack([np.cos(shift), np.sin(shift)]).astype(np.float32),
        coarse=(np.stack([np.cos(coarse), np.sin(coarse)], 1) / 32.0).astype(np.float32),
    )


PAIRS = [(128 * k, at, at + 256) for k, at in enumerate((0, 128, 512, 640))]
ODD_PAIRS = [(512 + 128 * k, 1024 + 128 * k, 1536 + 128 * k) for k in range(4)]
ALL_PAIRS = PAIRS + ODD_PAIRS


def split(values):
    high = values.astype(BF16)
    return high, (values - high.astype(F32)).astype(BF16)


def dot3(values, table, dims=NN):
    high, low = split(values) if not isinstance(values, tuple) else values
    dot = functools.partial(lax.dot_general, dimension_numbers=dims, preferred_element_type=F32)
    rows = high.shape[0]
    both = dot(jnp.concatenate([high, low], 0), table[0])
    return both[:rows] + (both[rows:] + dot(high, table[1]))


COLS = 1024


def spectrum(even, diff, seam, mix, nyquist, tail):
    real = jnp.concatenate([diff[:, :256], diff[:, 512:768]], 1)
    imag = jnp.concatenate([diff[:, 256:512], diff[:, 768:]], 1)
    added = dot3(seam[:, :16], (tail[0], tail[1]))
    even = even + added[:, :HALF]
    column = lax.broadcasted_iota(jnp.int32, even.shape, 1)
    even = jnp.where(column == 256, 0.0, even)
    total = jnp.where(
        lax.broadcasted_iota(jnp.int32, (diff.shape[0], 128), 1) == 0,
        imag[:, :128] - real[:, :128],
        0.0,
    )
    for part in range(4):
        total = total + 2.0 * real[:, 128 * part : 128 * part + 128]
    start = jnp.sum(total, axis=1, keepdims=True) * (1.0 / HALF)
    odd_im = dot3(real, (mix[0, 0], mix[0, 1])) + imag[:, :1] * nyquist[...]
    odd_re = dot3(imag, (mix[1, 0], mix[1, 1])) + start
    return jnp.concatenate(
        [even, odd_re + added[:, HALF : HALF + 512], odd_im + added[:, HALF + 512 :]], 1
    )


def whiten(values):
    power = jnp.zeros((values.shape[0], 128), F32)
    for part in range(16):
        piece = values[:, 128 * part : 128 * part + 128]
        power = power + piece * piece
    for step in (16, 32, 64):
        power = power + pltpu.roll(power, step, 1)
    factor = 1.0 / jnp.sqrt(power * (1.0 / 128.0) + 1e-06)
    return values * jnp.concatenate([factor] * 16, 1)


def first_section():
    return lax.axis_index("sec") == 0


def prepare_kernel(
    source_hbm, strain, offset_hbm, fir_hbm, dft_hbm, mix_hbm, nyquist_hbm, tail_hbm,
    msg_hbm, e32_hbm, e16_hbm, seam_hbm,
    source, offset, fir, dft, mix, nyquist, tail, msg, e16, seam_out, ext, dec, e32, sems, more,
):
    width = ext.shape[1]
    loads = []
    for part in range(strain.shape[1] // COLS):
        at = pl.ds(part * COLS, COLS)
        to = pl.ds(128 + part * COLS, COLS)
        loads.append(pltpu.make_async_copy(strain.at[:, at], ext.at[:, to], sems.at[part]))
    small = [(fir_hbm, fir), (offset_hbm, offset)]
    later = [
        (dft_hbm.at[0], dft.at[0]), (dft_hbm.at[1], dft.at[1]), (mix_hbm, mix),
        (nyquist_hbm, nyquist), (tail_hbm, tail), (source_hbm, source),
    ]
    fetch = [pltpu.make_async_copy(*ends, more.at[k]) for k, ends in enumerate(small + later)]
    for copy in fetch[:2] + loads + fetch[7:]:
        copy.start()
    ext[:, :128] = jnp.zeros((CH, 128), F32)
    ext[:, width - 128 :] = jnp.zeros((CH, 128), F32)
    lane = lax.broadcasted_iota(jnp.int32, (TAPS, 640), 1)
    tap = lax.broadcasted_iota(jnp.int32, (TAPS, 640), 0)
    place = jnp.where(lane + tap == 128, 1.0, 0.0).astype(F32)
    fetch[0].wait()
    row = lax.dot_general(
        jnp.broadcast_to(fir[...], (8, TAPS)),
        place,
        NN,
        precision=lax.Precision.HIGHEST,
        preferred_element_type=F32,
    )
    band = pltpu.roll(jnp.broadcast_to(row[:1], (128, 640)), 0, 1, stride=4, stride_axis=0)
    band = split(band)
    fetch[1].wait()
    off = jnp.broadcast_to(offset[...].astype(F32), (CH, CH)).T[:, :1]

    def filtered(start, length):
        raw = ext[:, start : min(start + length + 128, width)]
        size = raw.shape[1]
        raw = jnp.where(off >= 2.0, pltpu.roll(raw, size - 2, 1), raw)
        raw = jnp.where((off == 1.0) | (off == 3.0), pltpu.roll(raw, size - 1, 1), raw)
        return dot3(raw[:, :length], (band[0][:, :length], band[1][:, :length]), NT)

    for part, load in enumerate(loads):
        load.wait()
        if part == 1:
            for copy in fetch[2:7]:
                copy.start()
        for block in range(max(2 * part - 1, 0), 2 * part + 1):
            dec[:, 128 * block : 128 * block + 128] = filtered(512 * block, 640)
    dec[:, HALF - 128 :] = filtered(3584, 640)
    seam = jnp.where(first_section(), filtered(4096, 256), 0.0)
    seam_out[...] = seam
    first, second = dec[:, :512], dec[:, 512:]
    for quad, folded in enumerate((first + second, first - second)):
        fetch[2 + quad].wait()
        e32[:, 512 * quad : 512 * quad + 512] = dot3(folded, (dft[quad, 0], dft[quad, 1]))
    for part in range(8):
        at = slice(128 * part, 128 * part + 128)
        e16[at, :] = e32[:, at].astype(BF16)
    e16[HALF : HALF + 16, :] = seam.T[:16].astype(BF16)
    sends = [
        pltpu.make_async_copy(e32, e32_hbm, sems.at[0]),
        pltpu.make_async_copy(e16, e16_hbm, sems.at[1]),
        pltpu.make_async_copy(seam_out, seam_hbm, sems.at[2]),
        pltpu.make_async_copy(msg, msg_hbm, sems.at[3]),
    ]
    for copy in sends[:3]:
        copy.start()
    for copy in fetch[4:]:
        copy.wait()
    ids = [source[0], source[1]]
    even = jnp.concatenate([e32[pl.ds(src, 1), :] for src in ids] * 4, 0)
    edge = jnp.concatenate([seam_out[pl.ds(src, 1), :] for src in ids] * 4, 0)
    sign = jnp.where(first_section(), 1.0, -1.0).astype(F32)
    share = spectrum(even, even * sign, edge, mix, nyquist, tail)
    peers = msg.shape[0] // 2
    for slot in range(2):
        block = jnp.concatenate(
            [share[slot : slot + 1, 128 * part : 128 * part + 128] for part in range(16)], 0
        )
        for peer in range(peers):
            msg[peers * slot + peer] = block
    sends[3].start()
    for copy in sends:
        copy.wait()


def source_kernel(parts, out):
    count = parts.shape[0] // 2
    lines = [parts[:count, part, :] + parts[count:, part, :] for part in range(16)]
    white = whiten(jnp.concatenate([jnp.concatenate(lines, 1)] * 2, 0))
    rows = [
        white[k : k + 1, 128 * part : 128 * part + 128] for k in range(count) for part in range(16)
    ]
    block = jnp.concatenate(rows, 0).astype(BF16)
    for peer in range(out.shape[0]):
        out[peer] = block


def receiver_kernel(own_hbm, far, own_seam, mix, nyquist, tail, white, own, sem):
    load = pltpu.make_async_copy(own_hbm, own, sem)
    load.start()
    got = jnp.concatenate(
        [far[128 * part : 128 * part + 128, :].astype(F32) for part in range(8)], 1
    )
    got_seam = jnp.concatenate(
        [far[HALF : HALF + 16, :].astype(F32), jnp.zeros((112, 128), F32)], 0
    ).T
    load.wait()
    mine = own[...]
    sign = jnp.where(first_section(), 1.0, -1.0).astype(F32)
    seam = jnp.where(first_section(), own_seam[...], got_seam)
    white[...] = whiten(spectrum(mine + got, (mine - got) * sign, seam, mix, nyquist, tail))


LINES = 2
COUNT = 64
PART = 8
CHUNKS = NA // PART
SEND = 16


def turn_sources(chosen, shift, left, first, count, row):
    for two in range(count // 2):
        parts = [chosen[first + 2 * two + k].astype(F32) for k in range(2)]
        at = slice(row + 16 * two, row + 16 * two + 16)
        for col, re_at, im_at in ALL_PAIRS:
            cos = shift[0, :, col : col + 128]
            sin = shift[1, :, col : col + 128]
            up, low = re_at // 128, im_at // 128
            re = [jnp.broadcast_to(p[up : up + 1], (NB, 128)) for p in parts]
            im = [jnp.broadcast_to(p[low : low + 1], (NB, 128)) for p in parts]
            left[at, re_at : re_at + 128] = jnp.concatenate(
                [re[k] * cos + im[k] * sin for k in range(2)], 0
            ).astype(BF16)
            left[at, im_at : im_at + 128] = jnp.concatenate(
                [im[k] * cos - re[k] * sin for k in range(2)], 0
            ).astype(BF16)


def correlate_kernel(near, far, white, shift, coarse, out_hbm, *scratch):
    turned, rest = scratch[:CHUNKS], scratch[CHUNKS:]
    left, sums, (out, sems) = rest[:2], rest[2:4], rest[4:]
    each = COUNT // CHUNKS
    core = lax.rem(lax.axis_index("rcv"), 2)

    def turn(line, n):
        if line < LINES:
            turn_sources((near, far)[line], shift, left[line], n * each, each, n * each * NB)

    def build(n):
        if n >= CHUNKS:
            return
        for k in range(PART):
            a = n * PART + k
            at = slice(k * CH, k * CH + CH)
            for col, re_at, im_at in ALL_PAIRS:
                re = white[:, re_at : re_at + 128]
                im = white[:, im_at : im_at + 128]
                cos = coarse[a, 0:1, col : col + 128]
                sin = coarse[a, 1:2, col : col + 128]
                turned[n][at, re_at : re_at + 128] = (re * cos - im * sin).astype(BF16)
                turned[n][at, im_at : im_at + 128] = (re * sin + im * cos).astype(BF16)

    def product(line, n):
        total = lax.dot_general(left[line][...], turned[n][...], NT, preferred_element_type=F32)
        for k in range(PART):
            sums[line][n * PART + k] = total[:, CH * k : CH * k + CH]

    def finish(line, n):
        if line < 0:
            return
        for k in range(n * each, n * each + each):
            tile = sums[line][:, k * NB : k * NB + NB, :].reshape(NA * NB, CH)
            out[line, k // 16 * 16 + k % 4 * 4 + k % 16 // 4] = tile.T.astype(BF16)
            if (k + 1) % SEND == 0:
                send(line, k // SEND).start()

    def send(line, group):
        at = pl.ds(group * SEND, SEND)
        to = core if line == 0 else 1 - core
        sem = sems.at[line * (COUNT // SEND) + group]
        return pltpu.make_async_copy(out.at[line, at], out_hbm.at[at, to], sem)

    for n in range(CHUNKS):
        turn(0, n)
    build(0)
    for line in range(LINES):
        for n in range(CHUNKS):
            product(line, n)
            if line == 0:
                build(n + 1)
            turn(line + 1, n)
            finish(line - 1, n)
    for n in range(CHUNKS):
        finish(LINES - 1, n)
    for line in range(LINES):
        for group in range(COUNT // SEND):
            send(line, group).wait()


def vmem(count):
    return [pl.BlockSpec(memory_space=pltpu.VMEM)] * count


SMEM = pl.BlockSpec(memory_space=pltpu.SMEM)
HBM = pl.BlockSpec(memory_space=pltpu.HBM)


def limit(mib):
    return pltpu.CompilerParams(vmem_limit_bytes=mib * 2**20)


def cost(mega_flops, mib):
    return pl.CostEstimate(flops=mega_flops * 10**6, bytes_accessed=mib * 2**20, transcendentals=0)


def prepare(source, strain, offset, fir, tab):
    width = strain.shape[1] + 256
    constants = [tab["dft"], tab["mix"], tab["nyquist"], tab["tail"]]
    shapes = [
        ((8, 16, 128), F32),
        ((CH, HALF), F32),
        ((HALF + 16, 128), BF16),
        ((CH, 128), F32),
    ]
    return pl.pallas_call(
        prepare_kernel,
        out_shape=[jax.ShapeDtypeStruct(*s) for s in shapes],
        in_specs=[HBM] * 8,
        out_specs=[HBM] * 4,
        scratch_shapes=[
            pltpu.SMEM(source.shape, jnp.int32),
            pltpu.VMEM(offset.shape, jnp.int32),
            pltpu.VMEM(fir.shape, F32),
        ]
        + [pltpu.VMEM(t.shape, t.dtype) for t in constants]
        + [
            pltpu.VMEM((8, 16, 128), F32),
            pltpu.VMEM((HALF + 16, 128), BF16),
            pltpu.VMEM((CH, 128), F32),
            pltpu.VMEM((CH, width), F32),
            pltpu.VMEM((CH, HALF), F32),
            pltpu.VMEM((CH, HALF), F32),
            pltpu.SemaphoreType.DMA((strain.shape[1] // COLS,)),
            pltpu.SemaphoreType.DMA((8,)),
        ],
        compiler_params=limit(63),
        cost_estimate=cost(4000, 6),
        name="prepare",
    )(source, strain, offset, fir, *constants)


def finish_sources(parts, peers):
    return pl.pallas_call(
        source_kernel,
        out_shape=jax.ShapeDtypeStruct((peers, 64, 128), BF16),
        in_specs=vmem(1),
        out_specs=vmem(1)[0],
        compiler_params=limit(32),
        cost_estimate=cost(40000, 3),
        name="finish_sources",
    )(parts)


def finish_receivers(own, far, own_tail, tab):
    return pl.pallas_call(
        receiver_kernel,
        out_shape=jax.ShapeDtypeStruct((CH, TD), F32),
        in_specs=[HBM] + vmem(5),
        out_specs=vmem(1)[0],
        scratch_shapes=[pltpu.VMEM((CH, HALF), F32), pltpu.SemaphoreType.DMA],
        compiler_params=limit(32),
        cost_estimate=cost(3000, 6),
        name="finish_receivers",
    )(own, far, own_tail, tab["mix"], tab["nyquist"], tab["tail"])


def correlate(near, far, white, tab):
    return pl.pallas_call(
        correlate_kernel,
        out_shape=jax.ShapeDtypeStruct((COUNT, 2, CH, 128), BF16),
        in_specs=vmem(5),
        out_specs=HBM,
        scratch_shapes=[pltpu.VMEM((PART * CH, TD), BF16)] * CHUNKS
        + [pltpu.VMEM((COUNT * NB, TD), BF16)] * LINES
        + [pltpu.VMEM((NA, COUNT * NB, CH), F32)] * LINES
        + [
            pltpu.VMEM((LINES, COUNT, CH, 128), BF16),
            pltpu.SemaphoreType.DMA((LINES * COUNT // SEND,)),
        ],
        compiler_params=limit(32),
        cost_estimate=cost(9000, 13),
        name="correlate",
    )(near, far, white, tab["shift"], tab["coarse"])


def section_groups(size):
    y, z, x, core = SHAPE
    plane = x * core
    return [
        [s * size + (j * z + k) * plane + i for s in range(2) for k in range(z)]
        for j in range(y)
        for i in range(plane)
    ]


def plane_groups():
    y, z, x, core = SHAPE
    return [
        [((j * z + k) * x + i) * core + c for j in range(y) for i in range(x)]
        for k in range(z)
        for c in range(core)
    ]


def per_device(strain, offset, fir_taps, source_channel):
    tab = tables()
    size = lax.axis_size("rcv")
    msg, e32, e16, own_seam = prepare(
        source_channel, strain, offset[None, :], fir_taps[None, :], tab
    )
    parts = lax.all_to_all(msg, ("sec", "rcv"), 0, 0, axis_index_groups=section_groups(size))
    got16 = lax.ppermute(e16, "sec", [(0, 1), (1, 0)])
    groups = plane_groups()
    mine = finish_sources(parts, len(groups[0]))
    near = lax.all_to_all(mine, "rcv", 0, 0, axis_index_groups=groups)
    far = lax.ppermute(near, "rcv", [(k, k + 1 - 2 * (k % 2)) for k in range(size)])
    white = finish_receivers(e32, got16, own_seam, tab)
    out = correlate(near.reshape(COUNT, 16, 128), far.reshape(COUNT, 16, 128), white, tab)
    return out.reshape(1, 2 * COUNT, CH, 128)


def solution(mesh):
    in_specs = (P("rcv", "sec"), P("rcv"), P(), P("rcv"))
    out_specs = P("sec", None, "rcv", None)
    return jax.shard_map(
        per_device, mesh=mesh, in_specs=in_specs, out_specs=out_specs, check_vma=False
    )
```

```python
import functools

import jax
import jax.numpy as jnp
import ml_dtypes
import numpy as np
from jax import lax
from jax.experimental import pallas as pl
from jax.experimental.pallas import tpu as pltpu
from jax.sharding import PartitionSpec as P

TD = 2048
HALF = 1024
TAPS = 64
CH = 128
NA = 8
NB = 16
SHAPE = (4, 4, 4, 2)
NN = (((1,), (0,)), ((), ()))
NT = (((1,), (1,)), ((), ()))
F32 = jnp.float32
BF16 = jnp.bfloat16


def bins(first, step, count):
    col = np.arange(count)
    rank = col // 128 * 8 + col % 128 // 16
    return 64 * (col % 16) + step * rank + first


def split_table(table):
    high = table.astype(ml_dtypes.bfloat16)
    low = (table - high.astype(np.float64)).astype(ml_dtypes.bfloat16)
    return np.stack([high, low])


def cot(num):
    return 1.0 / np.tan(np.pi * num / TD)


def wave(freq, times):
    ang = 2 * np.pi * (freq[None, :] * times % TD) / TD
    return np.cos(ang), -np.sin(ang)


@functools.cache
def tables():
    quads = [bins(0, 4, 256), bins(2, 4, 256)]
    odd = bins(1, 2, 512)
    even = np.concatenate(quads)
    time = np.arange(512)[:, None]
    dft = []
    for freq in quads:
        re, im = wave(freq, time)
        if freq[0] == 0:
            im[:, 0] = (-1.0) ** np.arange(512)
        dft.append(split_table(np.concatenate([re, im], 1)))
    fe, fo = even[:, None], odd[None, :]
    norm = 2.0 / HALF
    re_im = -0.5 * (cot(fe + fo) + cot(fo - fe)) * np.where(fe == 0, 0.5 * norm, norm)
    im_re = -0.5 * (cot(fe + fo) + cot(fe - fo)) * np.where(fe == 0, 0.0, norm)
    nyquist = -0.5 * (cot(HALF + fo) + cot(fo - HALF)) / HALF
    rows = np.arange(16)[:, None]
    tail = np.concatenate(
        wave(quads[0], rows) + wave(quads[1], rows) + tuple(-w for w in wave(odd, rows)), 1
    )
    both = np.concatenate([even, odd])[None, :]
    shift = 2 * np.pi * (both * np.arange(NB)[:, None] % TD) / TD
    coarse = 2 * np.pi * (both * (NB * np.arange(NA)[:, None] - 64) % TD) / TD
    return dict(
        dft=np.stack(dft),
        mix=np.stack([split_table(re_im), split_table(im_re)]),
        nyquist=nyquist.astype(np.float32),
        tail=split_table(tail),
        shift=np.stack([np.cos(shift), np.sin(shift)]).astype(np.float32),
        coarse=(np.stack([np.cos(coarse), np.sin(coarse)], 1) / 32.0).astype(np.float32),
    )


PAIRS = [(128 * k, at, at + 256) for k, at in enumerate((0, 128, 512, 640))]
ODD_PAIRS = [(512 + 128 * k, 1024 + 128 * k, 1536 + 128 * k) for k in range(4)]
ALL_PAIRS = PAIRS + ODD_PAIRS


def split(values):
    high = values.astype(BF16)
    return high, (values - high.astype(F32)).astype(BF16)


def dot3(values, table, dims=NN):
    high, low = split(values) if not isinstance(values, tuple) else values
    dot = functools.partial(lax.dot_general, dimension_numbers=dims, preferred_element_type=F32)
    rows = high.shape[0]
    both = dot(jnp.concatenate([high, low], 0), table[0])
    return both[:rows] + (both[rows:] + dot(high, table[1]))


COLS = 2048


def spectrum(even, diff, seam, mix, nyquist, tail):
    real = jnp.concatenate([diff[:, :256], diff[:, 512:768]], 1)
    imag = jnp.concatenate([diff[:, 256:512], diff[:, 768:]], 1)
    added = dot3(seam[:, :16], (tail[0], tail[1]))
    even = even + added[:, :HALF]
    column = lax.broadcasted_iota(jnp.int32, even.shape, 1)
    even = jnp.where(column == 256, 0.0, even)
    total = jnp.where(
        lax.broadcasted_iota(jnp.int32, (diff.shape[0], 128), 1) == 0,
        imag[:, :128] - real[:, :128],
        0.0,
    )
    for part in range(4):
        total = total + 2.0 * real[:, 128 * part : 128 * part + 128]
    start = jnp.sum(total, axis=1, keepdims=True) * (1.0 / HALF)
    odd_im = dot3(real, (mix[0, 0], mix[0, 1])) + imag[:, :1] * nyquist[...]
    odd_re = dot3(imag, (mix[1, 0], mix[1, 1])) + start
    return jnp.concatenate(
        [even, odd_re + added[:, HALF : HALF + 512], odd_im + added[:, HALF + 512 :]], 1
    )


def whiten(values):
    power = jnp.zeros((values.shape[0], 128), F32)
    for part in range(16):
        piece = values[:, 128 * part : 128 * part + 128]
        power = power + piece * piece
    for step in (16, 32, 64):
        power = power + pltpu.roll(power, step, 1)
    factor = 1.0 / jnp.sqrt(power * (1.0 / 128.0) + 1e-06)
    return values * jnp.concatenate([factor] * 16, 1)


def first_section():
    return lax.axis_index("sec") == 0


def prepare_kernel(
    source_hbm, strain, offset_hbm, fir_hbm, dft_hbm, mix_hbm, nyquist_hbm, tail_hbm,
    msg_hbm, e32_hbm, e16_hbm, seam_hbm,
    source, offset, fir, dft, mix, nyquist, tail, msg, e16, seam_out, ext, dec, e32, sems, more,
):
    width = ext.shape[1]
    loads = []
    for part in range(strain.shape[1] // COLS):
        at = pl.ds(part * COLS, COLS)
        to = pl.ds(128 + part * COLS, COLS)
        loads.append(pltpu.make_async_copy(strain.at[:, at], ext.at[:, to], sems.at[part]))
    small = [(fir_hbm, fir), (offset_hbm, offset)]
    later = [
        (dft_hbm.at[0], dft.at[0]), (dft_hbm.at[1], dft.at[1]), (mix_hbm, mix),
        (nyquist_hbm, nyquist), (tail_hbm, tail), (source_hbm, source),
    ]
    fetch = [pltpu.make_async_copy(*ends, more.at[k]) for k, ends in enumerate(small + later)]
    for copy in fetch[:2] + loads + fetch[2:4] + fetch[7:]:
        copy.start()
    ext[:, :128] = jnp.zeros((CH, 128), F32)
    ext[:, width - 128 :] = jnp.zeros((CH, 128), F32)
    lane = lax.broadcasted_iota(jnp.int32, (TAPS, 640), 1)
    tap = lax.broadcasted_iota(jnp.int32, (TAPS, 640), 0)
    place = jnp.where(lane + tap == 128, 1.0, 0.0).astype(F32)
    fetch[0].wait()
    row = lax.dot_general(
        jnp.broadcast_to(fir[...], (8, TAPS)),
        place,
        NN,
        precision=lax.Precision.HIGHEST,
        preferred_element_type=F32,
    )
    band = pltpu.roll(jnp.broadcast_to(row[:1], (128, 640)), 0, 1, stride=4, stride_axis=0)
    band = split(band)
    fetch[1].wait()
    off = jnp.broadcast_to(offset[...].astype(F32), (CH, CH)).T[:, :1]

    def filtered(start, length):
        raw = ext[:, start : min(start + length + 128, width)]
        size = raw.shape[1]
        raw = jnp.where(off >= 2.0, pltpu.roll(raw, size - 2, 1), raw)
        raw = jnp.where((off == 1.0) | (off == 3.0), pltpu.roll(raw, size - 1, 1), raw)
        return dot3(raw[:, :length], (band[0][:, :length], band[1][:, :length]), NT)

    for part, load in enumerate(loads):
        load.wait()
        if part == 1:
            for copy in fetch[4:7]:
                copy.start()
        for block in range(max(4 * part - 1, 0), 4 * part + 3):
            dec[:, 128 * block : 128 * block + 128] = filtered(512 * block, 640)
    dec[:, HALF - 128 :] = filtered(3584, 640)
    seam = jnp.where(first_section(), filtered(4096, 256), 0.0)
    seam_out[...] = seam
    first, second = dec[:, :512], dec[:, 512:]
    for quad, folded in enumerate((first + second, first - second)):
        fetch[2 + quad].wait()
        e32[:, 512 * quad : 512 * quad + 512] = dot3(folded, (dft[quad, 0], dft[quad, 1]))
    for part in range(8):
        at = slice(128 * part, 128 * part + 128)
        e16[at, :] = e32[:, at].astype(BF16)
    e16[HALF : HALF + 16, :] = seam.T[:16].astype(BF16)
    sends = [
        pltpu.make_async_copy(e32, e32_hbm, sems.at[0]),
        pltpu.make_async_copy(e16, e16_hbm, sems.at[1]),
        pltpu.make_async_copy(seam_out, seam_hbm, sems.at[2]),
        pltpu.make_async_copy(msg, msg_hbm, sems.at[3]),
    ]
    for copy in sends[:3]:
        copy.start()
    for copy in fetch[4:]:
        copy.wait()
    ids = [source[0], source[1]]
    even = jnp.concatenate([e32[pl.ds(src, 1), :] for src in ids] * 4, 0)
    edge = jnp.concatenate([seam_out[pl.ds(src, 1), :] for src in ids] * 4, 0)
    sign = jnp.where(first_section(), 1.0, -1.0).astype(F32)
    share = spectrum(even, even * sign, edge, mix, nyquist, tail)
    peers = msg.shape[0] // 2
    for slot in range(2):
        block = jnp.concatenate(
            [share[slot : slot + 1, 128 * part : 128 * part + 128] for part in range(16)], 0
        )
        for peer in range(peers):
            msg[peers * slot + peer] = block
    sends[3].start()
    for copy in sends:
        copy.wait()


def source_kernel(parts, out):
    count = parts.shape[0] // 2
    lines = [parts[:count, part, :] + parts[count:, part, :] for part in range(16)]
    white = whiten(jnp.concatenate([jnp.concatenate(lines, 1)] * 2, 0))
    rows = [
        white[k : k + 1, 128 * part : 128 * part + 128] for k in range(count) for part in range(16)
    ]
    block = jnp.concatenate(rows, 0).astype(BF16)
    for peer in range(out.shape[0]):
        out[peer] = block


def receiver_kernel(own_hbm, far, own_seam, mix, nyquist, tail, white, own, sem):
    load = pltpu.make_async_copy(own_hbm, own, sem)
    load.start()
    got = jnp.concatenate(
        [far[128 * part : 128 * part + 128, :].astype(F32) for part in range(8)], 1
    )
    got_seam = jnp.concatenate(
        [far[HALF : HALF + 16, :].astype(F32), jnp.zeros((112, 128), F32)], 0
    ).T
    load.wait()
    mine = own[...]
    sign = jnp.where(first_section(), 1.0, -1.0).astype(F32)
    seam = jnp.where(first_section(), own_seam[...], got_seam)
    white[...] = whiten(spectrum(mine + got, (mine - got) * sign, seam, mix, nyquist, tail))


COUNT = 64
LINE = 64
LINES = 2 * COUNT // LINE
PART = 4
CHUNKS = NA // PART
SEND = 8


def turn_sources(chosen, shift, left, first, count, row):
    for k in range(count):
        values = chosen[first + k].astype(F32)
        at = slice(row + NB * k, row + NB * k + NB)
        for col, re_at, im_at in ALL_PAIRS:
            cos = shift[0, :, col : col + 128]
            sin = shift[1, :, col : col + 128]
            up, low = re_at // 128, im_at // 128
            re = jnp.broadcast_to(values[up : up + 1], (NB, 128))
            im = jnp.broadcast_to(values[low : low + 1], (NB, 128))
            left[at, re_at : re_at + 128] = (re * cos + im * sin).astype(BF16)
            left[at, im_at : im_at + 128] = (im * cos - re * sin).astype(BF16)


def correlate_kernel(near, far, white, shift, coarse, out_hbm, *scratch):
    turned, rest = scratch[:CHUNKS], scratch[CHUNKS:]
    left, sums, (out, sems) = rest[:2], rest[2:4], rest[4:]
    each = LINE // CHUNKS
    core = lax.rem(lax.axis_index("rcv"), 2)

    def place(line):
        return line * LINE // COUNT, line * LINE % COUNT

    def turn(line, n):
        if line < LINES:
            side, first = place(line)
            turn_sources(
                (near, far)[side], shift, left[line % 2], first + n * each, each, n * each * NB
            )

    def build(n):
        if n >= CHUNKS:
            return
        for k in range(PART):
            a = n * PART + k
            at = slice(k * CH, k * CH + CH)
            for col, re_at, im_at in ALL_PAIRS:
                re = white[:, re_at : re_at + 128]
                im = white[:, im_at : im_at + 128]
                cos = coarse[a, 0:1, col : col + 128]
                sin = coarse[a, 1:2, col : col + 128]
                turned[n][at, re_at : re_at + 128] = (re * cos - im * sin).astype(BF16)
                turned[n][at, im_at : im_at + 128] = (re * sin + im * cos).astype(BF16)

    def product(line, n):
        total = lax.dot_general(
            left[line % 2][...], turned[n][...], NT, preferred_element_type=F32
        )
        for k in range(PART):
            sums[line % 2][n * PART + k] = total[:, CH * k : CH * k + CH]

    def finish(line, n):
        if line < 0:
            return
        side, first = place(line)
        for k in range(n * each, n * each + each):
            row = (k // 16 * 16 + k % 4 * 4 + k % 16 // 4) * NB
            tile = sums[line % 2][:, row : row + NB, :].reshape(NA * NB, CH)
            out[side, first + k] = tile.T.astype(BF16)
            if (k + 1) % SEND == 0:
                send(side, (first + k) // SEND).start()

    def send(side, group):
        at = pl.ds(group * SEND, SEND)
        to = core if side == 0 else 1 - core
        sem = sems.at[side * (COUNT // SEND) + group]
        return pltpu.make_async_copy(out.at[side, at], out_hbm.at[at, to], sem)

    for n in range(CHUNKS):
        turn(0, n)
    build(0)
    for line in range(LINES):
        for n in range(CHUNKS):
            product(line, n)
            if line == 0:
                build(n + 1)
            turn(line + 1, n)
            finish(line - 1, n)
    for n in range(CHUNKS):
        finish(LINES - 1, n)
    for side in range(2):
        for group in range(COUNT // SEND):
            send(side, group).wait()


def vmem(count):
    return [pl.BlockSpec(memory_space=pltpu.VMEM)] * count


SMEM = pl.BlockSpec(memory_space=pltpu.SMEM)
HBM = pl.BlockSpec(memory_space=pltpu.HBM)


def limit(mib):
    return pltpu.CompilerParams(vmem_limit_bytes=mib * 2**20)


def cost(mega_flops, mib):
    return pl.CostEstimate(flops=mega_flops * 10**6, bytes_accessed=mib * 2**20, transcendentals=0)


def prepare(source, strain, offset, fir, tab):
    width = strain.shape[1] + 256
    constants = [tab["dft"], tab["mix"], tab["nyquist"], tab["tail"]]
    shapes = [
        ((8, 16, 128), F32),
        ((CH, HALF), F32),
        ((HALF + 16, 128), BF16),
        ((CH, 128), F32),
    ]
    return pl.pallas_call(
        prepare_kernel,
        out_shape=[jax.ShapeDtypeStruct(*s) for s in shapes],
        in_specs=[HBM] * 8,
        out_specs=[HBM] * 4,
        scratch_shapes=[
            pltpu.SMEM(source.shape, jnp.int32),
            pltpu.VMEM(offset.shape, jnp.int32),
            pltpu.VMEM(fir.shape, F32),
        ]
        + [pltpu.VMEM(t.shape, t.dtype) for t in constants]
        + [
            pltpu.VMEM((8, 16, 128), F32),
            pltpu.VMEM((HALF + 16, 128), BF16),
            pltpu.VMEM((CH, 128), F32),
            pltpu.VMEM((CH, width), F32),
            pltpu.VMEM((CH, HALF), F32),
            pltpu.VMEM((CH, HALF), F32),
            pltpu.SemaphoreType.DMA((4,)),
            pltpu.SemaphoreType.DMA((8,)),
        ],
        compiler_params=limit(63),
        cost_estimate=cost(4000, 6),
        name="prepare",
    )(source, strain, offset, fir, *constants)


def finish_sources(parts, peers):
    return pl.pallas_call(
        source_kernel,
        out_shape=jax.ShapeDtypeStruct((peers, 64, 128), BF16),
        in_specs=vmem(1),
        out_specs=vmem(1)[0],
        compiler_params=limit(32),
        cost_estimate=cost(40000, 3),
        name="finish_sources",
    )(parts)


def finish_receivers(own, far, own_tail, tab):
    return pl.pallas_call(
        receiver_kernel,
        out_shape=jax.ShapeDtypeStruct((CH, TD), F32),
        in_specs=[HBM] + vmem(5),
        out_specs=vmem(1)[0],
        scratch_shapes=[pltpu.VMEM((CH, HALF), F32), pltpu.SemaphoreType.DMA],
        compiler_params=limit(32),
        cost_estimate=cost(3000, 6),
        name="finish_receivers",
    )(own, far, own_tail, tab["mix"], tab["nyquist"], tab["tail"])


def correlate(near, far, white, tab):
    return pl.pallas_call(
        correlate_kernel,
        out_shape=jax.ShapeDtypeStruct((COUNT, 2, CH, 128), BF16),
        in_specs=vmem(5),
        out_specs=HBM,
        scratch_shapes=[pltpu.VMEM((PART * CH, TD), BF16)] * CHUNKS
        + [pltpu.VMEM((LINE * NB, TD), BF16)] * 2
        + [pltpu.VMEM((NA, LINE * NB, CH), F32)] * 2
        + [
            pltpu.VMEM((2, COUNT, CH, 128), BF16),
            pltpu.SemaphoreType.DMA((2 * COUNT // SEND,)),
        ],
        compiler_params=limit(32),
        cost_estimate=cost(9000, 13),
        name="correlate",
    )(near, far, white, tab["shift"], tab["coarse"])


def section_groups(size):
    y, z, x, core = SHAPE
    plane = x * core
    return [
        [s * size + (j * z + k) * plane + i for s in range(2) for k in range(z)]
        for j in range(y)
        for i in range(plane)
    ]


def plane_groups():
    y, z, x, core = SHAPE
    return [
        [((j * z + k) * x + i) * core + c for j in range(y) for i in range(x)]
        for k in range(z)
        for c in range(core)
    ]


def per_device(strain, offset, fir_taps, source_channel):
    tab = tables()
    size = lax.axis_size("rcv")
    msg, e32, e16, own_seam = prepare(
        source_channel, strain, offset[None, :], fir_taps[None, :], tab
    )
    parts = lax.all_to_all(msg, ("sec", "rcv"), 0, 0, axis_index_groups=section_groups(size))
    got16 = lax.ppermute(e16, "sec", [(0, 1), (1, 0)])
    groups = plane_groups()
    mine = finish_sources(parts, len(groups[0]))
    near = lax.all_to_all(mine, "rcv", 0, 0, axis_index_groups=groups)
    far = lax.ppermute(near, "rcv", [(k, k + 1 - 2 * (k % 2)) for k in range(size)])
    white = finish_receivers(e32, got16, own_seam, tab)
    out = correlate(near.reshape(COUNT, 16, 128), far.reshape(COUNT, 16, 128), white, tab)
    return out.reshape(1, 2 * COUNT, CH, 128)


def solution(mesh):
    in_specs = (P("rcv", "sec"), P("rcv"), P(), P("rcv"))
    out_specs = P("sec", None, "rcv", None)
    return jax.shard_map(
        per_device, mesh=mesh, in_specs=in_specs, out_specs=out_specs, check_vma=False
    )
```

```python
import functools

import jax
import jax.numpy as jnp
import ml_dtypes
import numpy as np
from jax import lax
from jax.experimental import pallas as pl
from jax.experimental.pallas import tpu as pltpu
from jax.sharding import PartitionSpec as P

TD = 2048
HALF = 1024
TAPS = 64
CH = 128
NA = 8
NB = 16
SHAPE = (4, 4, 4, 2)
NN = (((1,), (0,)), ((), ()))
NT = (((1,), (1,)), ((), ()))
F32 = jnp.float32
BF16 = jnp.bfloat16


def bins(first, step, count):
    col = np.arange(count)
    rank = col // 128 * 8 + col % 128 // 16
    return 64 * (col % 16) + step * rank + first


def split_table(table):
    high = table.astype(ml_dtypes.bfloat16)
    low = (table - high.astype(np.float64)).astype(ml_dtypes.bfloat16)
    return np.stack([high, low])


def cot(num):
    return 1.0 / np.tan(np.pi * num / TD)


def wave(freq, times):
    ang = 2 * np.pi * (freq[None, :] * times % TD) / TD
    return np.cos(ang), -np.sin(ang)


@functools.cache
def tables():
    quads = [bins(0, 4, 256), bins(2, 4, 256)]
    odd = bins(1, 2, 512)
    even = np.concatenate(quads)
    time = np.arange(512)[:, None]
    dft = []
    for freq in quads:
        re, im = wave(freq, time)
        if freq[0] == 0:
            im[:, 0] = (-1.0) ** np.arange(512)
        dft.append(split_table(np.concatenate([re, im], 1)))
    fe, fo = even[:, None], odd[None, :]
    norm = 2.0 / HALF
    re_im = -0.5 * (cot(fe + fo) + cot(fo - fe)) * np.where(fe == 0, 0.5 * norm, norm)
    im_re = -0.5 * (cot(fe + fo) + cot(fe - fo)) * np.where(fe == 0, 0.0, norm)
    nyquist = -0.5 * (cot(HALF + fo) + cot(fo - HALF)) / HALF
    rows = np.arange(16)[:, None]
    tail = np.concatenate(
        wave(quads[0], rows) + wave(quads[1], rows) + tuple(-w for w in wave(odd, rows)), 1
    )
    both = np.concatenate([even, odd])[None, :]
    shift = 2 * np.pi * (both * np.arange(NB)[:, None] % TD) / TD
    coarse = 2 * np.pi * (both * (NB * np.arange(NA)[:, None] - 64) % TD) / TD
    return dict(
        dft=np.stack(dft),
        mix=np.stack([split_table(re_im), split_table(im_re)]),
        nyquist=nyquist.astype(np.float32),
        tail=split_table(tail),
        shift=np.stack([np.cos(shift), np.sin(shift)]).astype(np.float32),
        coarse=(np.stack([np.cos(coarse), np.sin(coarse)], 1) / 32.0).astype(np.float32),
    )


PAIRS = [(128 * k, at, at + 256) for k, at in enumerate((0, 128, 512, 640))]
ODD_PAIRS = [(512 + 128 * k, 1024 + 128 * k, 1536 + 128 * k) for k in range(4)]
ALL_PAIRS = PAIRS + ODD_PAIRS


def split(values):
    high = values.astype(BF16)
    return high, (values - high.astype(F32)).astype(BF16)


def dot3(values, table, dims=NN):
    high, low = split(values) if not isinstance(values, tuple) else values
    dot = functools.partial(lax.dot_general, dimension_numbers=dims, preferred_element_type=F32)
    rows = high.shape[0]
    both = dot(jnp.concatenate([high, low], 0), table[0])
    return both[:rows] + (both[rows:] + dot(high, table[1]))


COLS = 2048


def spectrum(even, diff, seam, mix, nyquist, tail):
    real = jnp.concatenate([diff[:, :256], diff[:, 512:768]], 1)
    imag = jnp.concatenate([diff[:, 256:512], diff[:, 768:]], 1)
    added = dot3(seam[:, :16], (tail[0], tail[1]))
    even = even + added[:, :HALF]
    column = lax.broadcasted_iota(jnp.int32, even.shape, 1)
    even = jnp.where(column == 256, 0.0, even)
    total = jnp.where(
        lax.broadcasted_iota(jnp.int32, (diff.shape[0], 128), 1) == 0,
        imag[:, :128] - real[:, :128],
        0.0,
    )
    for part in range(4):
        total = total + 2.0 * real[:, 128 * part : 128 * part + 128]
    start = jnp.sum(total, axis=1, keepdims=True) * (1.0 / HALF)
    odd_im = dot3(real, (mix[0, 0], mix[0, 1])) + imag[:, :1] * nyquist[...]
    odd_re = dot3(imag, (mix[1, 0], mix[1, 1])) + start
    return jnp.concatenate(
        [even, odd_re + added[:, HALF : HALF + 512], odd_im + added[:, HALF + 512 :]], 1
    )


def whiten(values):
    power = jnp.zeros((values.shape[0], 128), F32)
    for part in range(16):
        piece = values[:, 128 * part : 128 * part + 128]
        power = power + piece * piece
    for step in (16, 32, 64):
        power = power + pltpu.roll(power, step, 1)
    factor = 1.0 / jnp.sqrt(power * (1.0 / 128.0) + 1e-06)
    return values * jnp.concatenate([factor] * 16, 1)


def first_section():
    return lax.axis_index("sec") == 0


def prepare_kernel(
    source_hbm, strain, offset_hbm, fir_hbm, dft_hbm, mix_hbm, nyquist_hbm, tail_hbm,
    msg_hbm, e32_hbm, e16_hbm, seam_hbm,
    source, offset, fir, dft, mix, nyquist, tail, msg, e16, seam_out, ext, dec, e32, sems, more,
):
    width = ext.shape[1]
    loads = []
    for part in range(strain.shape[1] // COLS):
        at = pl.ds(part * COLS, COLS)
        to = pl.ds(128 + part * COLS, COLS)
        loads.append(
            [
                pltpu.make_async_copy(
                    strain.at[pl.ds(64 * h, 64), at], ext.at[pl.ds(64 * h, 64), to], sems.at[2 * part + h]
                )
                for h in range(2)
            ]
        )
    small = [(fir_hbm, fir), (offset_hbm, offset)]
    later = [
        (dft_hbm.at[0], dft.at[0]), (dft_hbm.at[1], dft.at[1]), (mix_hbm, mix),
        (nyquist_hbm, nyquist), (tail_hbm, tail), (source_hbm, source),
    ]
    fetch = [pltpu.make_async_copy(*ends, more.at[k]) for k, ends in enumerate(small + later)]
    for copy in fetch[:2] + loads[0] + loads[1] + fetch[2:4] + fetch[7:]:
        copy.start()
    ext[:, :128] = jnp.zeros((CH, 128), F32)
    ext[:, width - 128 :] = jnp.zeros((CH, 128), F32)
    lane = lax.broadcasted_iota(jnp.int32, (TAPS, 640), 1)
    tap = lax.broadcasted_iota(jnp.int32, (TAPS, 640), 0)
    place = jnp.where(lane + tap == 128, 1.0, 0.0).astype(F32)
    fetch[0].wait()
    row = lax.dot_general(
        jnp.broadcast_to(fir[...], (8, TAPS)),
        place,
        NN,
        precision=lax.Precision.HIGHEST,
        preferred_element_type=F32,
    )
    band = pltpu.roll(jnp.broadcast_to(row[:1], (128, 640)), 0, 1, stride=4, stride_axis=0)
    band = split(band)
    fetch[1].wait()
    off = jnp.broadcast_to(offset[...].astype(F32), (CH, CH)).T[:, :1]

    def filtered(start, length):
        raw = ext[:, start : min(start + length + 128, width)]
        size = raw.shape[1]
        raw = jnp.where(off >= 2.0, pltpu.roll(raw, size - 2, 1), raw)
        raw = jnp.where((off == 1.0) | (off == 3.0), pltpu.roll(raw, size - 1, 1), raw)
        return dot3(raw[:, :length], (band[0][:, :length], band[1][:, :length]), NT)

    for part, load in enumerate(loads):
        for copy in load:
            copy.wait()
        if part == 1:
            for copy in fetch[4:7]:
                copy.start()
        for block in range(max(4 * part - 1, 0), 4 * part + 3):
            dec[:, 128 * block : 128 * block + 128] = filtered(512 * block, 640)
    dec[:, HALF - 128 :] = filtered(3584, 640)
    seam = jnp.where(first_section(), filtered(4096, 256), 0.0)
    seam_out[...] = seam
    first, second = dec[:, :512], dec[:, 512:]
    for quad, folded in enumerate((first + second, first - second)):
        fetch[2 + quad].wait()
        e32[:, 512 * quad : 512 * quad + 512] = dot3(folded, (dft[quad, 0], dft[quad, 1]))
    for part in range(8):
        at = slice(128 * part, 128 * part + 128)
        e16[at, :] = e32[:, at].astype(BF16)
    e16[HALF : HALF + 16, :] = seam.T[:16].astype(BF16)
    sends = [
        pltpu.make_async_copy(e32, e32_hbm, sems.at[0]),
        pltpu.make_async_copy(e16, e16_hbm, sems.at[1]),
        pltpu.make_async_copy(seam_out, seam_hbm, sems.at[2]),
        pltpu.make_async_copy(msg, msg_hbm, sems.at[3]),
    ]
    for copy in sends[:3]:
        copy.start()
    for copy in fetch[4:]:
        copy.wait()
    ids = [source[0], source[1]]
    even = jnp.concatenate([e32[pl.ds(src, 1), :] for src in ids] * 4, 0)
    edge = jnp.concatenate([seam_out[pl.ds(src, 1), :] for src in ids] * 4, 0)
    sign = jnp.where(first_section(), 1.0, -1.0).astype(F32)
    share = spectrum(even, even * sign, edge, mix, nyquist, tail)
    peers = msg.shape[0] // 2
    for slot in range(2):
        block = jnp.concatenate(
            [share[slot : slot + 1, 128 * part : 128 * part + 128] for part in range(16)], 0
        )
        for peer in range(peers):
            msg[peers * slot + peer] = block
    sends[3].start()
    for copy in sends:
        copy.wait()


def source_kernel(parts, out):
    count = parts.shape[0] // 2
    lines = [parts[:count, part, :] + parts[count:, part, :] for part in range(16)]
    white = whiten(jnp.concatenate([jnp.concatenate(lines, 1)] * 2, 0))
    rows = [
        white[k : k + 1, 128 * part : 128 * part + 128] for k in range(count) for part in range(16)
    ]
    block = jnp.concatenate(rows, 0).astype(BF16)
    for peer in range(out.shape[0]):
        out[peer] = block


def receiver_kernel(own_hbm, far, own_seam, mix, nyquist, tail, white, own, sem):
    load = pltpu.make_async_copy(own_hbm, own, sem)
    load.start()
    got = jnp.concatenate(
        [far[128 * part : 128 * part + 128, :].astype(F32) for part in range(8)], 1
    )
    got_seam = jnp.concatenate(
        [far[HALF : HALF + 16, :].astype(F32), jnp.zeros((112, 128), F32)], 0
    ).T
    load.wait()
    mine = own[...]
    sign = jnp.where(first_section(), 1.0, -1.0).astype(F32)
    seam = jnp.where(first_section(), own_seam[...], got_seam)
    white[...] = whiten(spectrum(mine + got, (mine - got) * sign, seam, mix, nyquist, tail))


COUNT = 64
LINE = 64
LINES = 2 * COUNT // LINE
PART = 4
CHUNKS = NA // PART
SEND = 8


def turn_sources(chosen, shift, left, first, count, row):
    for k in range(count):
        values = chosen[first + k].astype(F32)
        at = slice(row + NB * k, row + NB * k + NB)
        for col, re_at, im_at in ALL_PAIRS:
            cos = shift[0, :, col : col + 128]
            sin = shift[1, :, col : col + 128]
            up, low = re_at // 128, im_at // 128
            re = jnp.broadcast_to(values[up : up + 1], (NB, 128))
            im = jnp.broadcast_to(values[low : low + 1], (NB, 128))
            left[at, re_at : re_at + 128] = (re * cos + im * sin).astype(BF16)
            left[at, im_at : im_at + 128] = (im * cos - re * sin).astype(BF16)


def correlate_kernel(near, far, white, shift, coarse, out_hbm, *scratch):
    turned, rest = scratch[:CHUNKS], scratch[CHUNKS:]
    left, sums, (out, sems) = rest[:2], rest[2:4], rest[4:]
    each = LINE // CHUNKS
    core = lax.rem(lax.axis_index("rcv"), 2)

    def place(line):
        return line * LINE // COUNT, line * LINE % COUNT

    def turn(line, n):
        if line < LINES:
            side, first = place(line)
            turn_sources(
                (near, far)[side], shift, left[line % 2], first + n * each, each, n * each * NB
            )

    def build(n):
        if n >= CHUNKS:
            return
        for k in range(PART):
            a = n * PART + k
            at = slice(k * CH, k * CH + CH)
            for col, re_at, im_at in ALL_PAIRS:
                re = white[:, re_at : re_at + 128]
                im = white[:, im_at : im_at + 128]
                cos = coarse[a, 0:1, col : col + 128]
                sin = coarse[a, 1:2, col : col + 128]
                turned[n][at, re_at : re_at + 128] = (re * cos - im * sin).astype(BF16)
                turned[n][at, im_at : im_at + 128] = (re * sin + im * cos).astype(BF16)

    def product(line, n):
        total = lax.dot_general(
            left[line % 2][...], turned[n][...], NT, preferred_element_type=F32
        )
        for k in range(PART):
            sums[line % 2][n * PART + k] = total[:, CH * k : CH * k + CH]

    def finish(line, n):
        if line < 0:
            return
        side, first = place(line)
        for k in range(n * each, n * each + each):
            row = (k // 16 * 16 + k % 4 * 4 + k % 16 // 4) * NB
            tile = sums[line % 2][:, row : row + NB, :].reshape(NA * NB, CH)
            out[side, first + k] = tile.T.astype(BF16)
            if (k + 1) % SEND == 0:
                send(side, (first + k) // SEND).start()

    def send(side, group):
        at = pl.ds(group * SEND, SEND)
        to = core if side == 0 else 1 - core
        sem = sems.at[side * (COUNT // SEND) + group]
        return pltpu.make_async_copy(out.at[side, at], out_hbm.at[at, to], sem)

    for n in range(CHUNKS):
        turn(0, n)
    build(0)
    for line in range(LINES):
        for n in range(CHUNKS):
            product(line, n)
            if line == 0:
                build(n + 1)
            turn(line + 1, n)
            finish(line - 1, n)
    for n in range(CHUNKS):
        finish(LINES - 1, n)
    for side in range(2):
        for group in range(COUNT // SEND):
            send(side, group).wait()


def vmem(count):
    return [pl.BlockSpec(memory_space=pltpu.VMEM)] * count


SMEM = pl.BlockSpec(memory_space=pltpu.SMEM)
HBM = pl.BlockSpec(memory_space=pltpu.HBM)


def limit(mib):
    return pltpu.CompilerParams(vmem_limit_bytes=mib * 2**20)


def cost(mega_flops, mib):
    return pl.CostEstimate(flops=mega_flops * 10**6, bytes_accessed=mib * 2**20, transcendentals=0)


def prepare(source, strain, offset, fir, tab):
    width = strain.shape[1] + 256
    constants = [tab["dft"], tab["mix"], tab["nyquist"], tab["tail"]]
    shapes = [
        ((8, 16, 128), F32),
        ((CH, HALF), F32),
        ((HALF + 16, 128), BF16),
        ((CH, 128), F32),
    ]
    return pl.pallas_call(
        prepare_kernel,
        out_shape=[jax.ShapeDtypeStruct(*s) for s in shapes],
        in_specs=[HBM] * 8,
        out_specs=[HBM] * 4,
        scratch_shapes=[
            pltpu.SMEM(source.shape, jnp.int32),
            pltpu.VMEM(offset.shape, jnp.int32),
            pltpu.VMEM(fir.shape, F32),
        ]
        + [pltpu.VMEM(t.shape, t.dtype) for t in constants]
        + [
            pltpu.VMEM((8, 16, 128), F32),
            pltpu.VMEM((HALF + 16, 128), BF16),
            pltpu.VMEM((CH, 128), F32),
            pltpu.VMEM((CH, width), F32),
            pltpu.VMEM((CH, HALF), F32),
            pltpu.VMEM((CH, HALF), F32),
            pltpu.SemaphoreType.DMA((4,)),
            pltpu.SemaphoreType.DMA((8,)),
        ],
        compiler_params=limit(63),
        cost_estimate=cost(4000, 6),
        name="prepare",
    )(source, strain, offset, fir, *constants)


def finish_sources(parts, peers):
    return pl.pallas_call(
        source_kernel,
        out_shape=jax.ShapeDtypeStruct((peers, 64, 128), BF16),
        in_specs=vmem(1),
        out_specs=vmem(1)[0],
        compiler_params=limit(32),
        cost_estimate=cost(40000, 3),
        name="finish_sources",
    )(parts)


def finish_receivers(own, far, own_tail, tab):
    return pl.pallas_call(
        receiver_kernel,
        out_shape=jax.ShapeDtypeStruct((CH, TD), F32),
        in_specs=[HBM] + vmem(5),
        out_specs=vmem(1)[0],
        scratch_shapes=[pltpu.VMEM((CH, HALF), F32), pltpu.SemaphoreType.DMA],
        compiler_params=limit(32),
        cost_estimate=cost(3000, 6),
        name="finish_receivers",
    )(own, far, own_tail, tab["mix"], tab["nyquist"], tab["tail"])


def correlate(near, far, white, tab):
    return pl.pallas_call(
        correlate_kernel,
        out_shape=jax.ShapeDtypeStruct((COUNT, 2, CH, 128), BF16),
        in_specs=vmem(5),
        out_specs=HBM,
        scratch_shapes=[pltpu.VMEM((PART * CH, TD), BF16)] * CHUNKS
        + [pltpu.VMEM((LINE * NB, TD), BF16)] * 2
        + [pltpu.VMEM((NA, LINE * NB, CH), F32)] * 2
        + [
            pltpu.VMEM((2, COUNT, CH, 128), BF16),
            pltpu.SemaphoreType.DMA((2 * COUNT // SEND,)),
        ],
        compiler_params=limit(32),
        cost_estimate=cost(9000, 13),
        name="correlate",
    )(near, far, white, tab["shift"], tab["coarse"])


def section_groups(size):
    y, z, x, core = SHAPE
    plane = x * core
    return [
        [s * size + (j * z + k) * plane + i for s in range(2) for k in range(z)]
        for j in range(y)
        for i in range(plane)
    ]


def plane_groups():
    y, z, x, core = SHAPE
    return [
        [((j * z + k) * x + i) * core + c for j in range(y) for i in range(x)]
        for k in range(z)
        for c in range(core)
    ]


def per_device(strain, offset, fir_taps, source_channel):
    tab = tables()
    size = lax.axis_size("rcv")
    msg, e32, e16, own_seam = prepare(
        source_channel, strain, offset[None, :], fir_taps[None, :], tab
    )
    parts = lax.all_to_all(msg, ("sec", "rcv"), 0, 0, axis_index_groups=section_groups(size))
    got16 = lax.ppermute(e16, "sec", [(0, 1), (1, 0)])
    groups = plane_groups()
    mine = finish_sources(parts, len(groups[0]))
    near = lax.all_to_all(mine, "rcv", 0, 0, axis_index_groups=groups)
    far = lax.ppermute(near, "rcv", [(k, k + 1 - 2 * (k % 2)) for k in range(size)])
    white = finish_receivers(e32, got16, own_seam, tab)
    out = correlate(near.reshape(COUNT, 16, 128), far.reshape(COUNT, 16, 128), white, tab)
    return out.reshape(1, 2 * COUNT, CH, 128)


def solution(mesh):
    in_specs = (P("rcv", "sec"), P("rcv"), P(), P("rcv"))
    out_specs = P("sec", None, "rcv", None)
    return jax.shard_map(
        per_device, mesh=mesh, in_specs=in_specs, out_specs=out_specs, check_vma=False
    )
```
